32 devices in a mesh: rep: 2 (over x), pool: 16 (over z, y, core).
Axes of the slice: x: 2, y: 2, z: 4, core: 2. Of those that a mesh axis runs over, the one named last changes fastest.
Arguments:
- hidden_state: bfloat16 [256, 6144], P(('rep', 'pool')), parts along dimension 0, may hold values from -80 to 80
- queries: bfloat16 [256, 6144], P(('rep', 'pool')), parts along dimension 0, may hold values from -100 to 100
- new_entries: bfloat16 [256, 2, 1024], P(('rep', 'pool')), parts along dimension 0, may hold values from -5 to 5
- cached: bfloat16 [4096, 2, 1024], P(('rep', 'pool')), parts along dimension 0, may hold values from -6 to 6
- cache_lengths: int32 [32, 8], P(('rep', 'pool')), parts along dimension 0, may hold values from 1 to 64, 128 in all within a row
- routes: int32 [256, 4], P(('rep', 'pool')), parts along dimension 0, may hold values from 0 to 15, all different within a row; in each aligned block of 8 rows (0 to 7, 8 to 15, ...) at most 4 rows name the same one
- norm_gain: float32 [6144], replicated, may hold values from 0.25 to 1.75
- router_weight: bfloat16 [6144, 16], replicated, may hold values from -0.078125 to 0.078125
- expert_gate: bfloat16 [16, 6144, 1344], P('pool'), may hold values from -0.078125 to 0.078125
- expert_up: bfloat16 [16, 6144, 1344], P('pool'), may hold values from -0.078125 to 0.078125
- expert_down: bfloat16 [16, 1344, 6144], P('pool'), may hold values from -0.0625 to 0.0625
Outputs:
- mixed: bfloat16 [256, 6144], P(('rep', 'pool')), parts along dimension 0
The draws below stay inside these ranges and needn't reach their ends.
There are 2 independent parts, one for each index of `rep`. The reference program is written for one: setup_inputs(seed, part) draws one part's arguments, and reference() takes and returns one part's arrays. A program takes and returns all parts, laid end to end along the dimension named above; an argument that names none is the same for every part. Nothing has to cross between parts.
Inputs may be any that keep to these rules, and one draw needn't show every extreme that they name: `routes`: each row names 4 different experts; the rows of one device name no expert more than 4 times. `cache_lengths`: the 8 lengths of a device sum to 128.
All inputs are finite; a program needn't handle non-finite values.
Results may differ from the reference program's by a relative error of at most 0.004.
Values may be sent and summed in bfloat16 or wider, within the bound.
No kernel may reach another device: no remote copies, remote signals or barrier semaphores. Data moves between devices by JAX's collectives and lax.ppermute only.
A program may use at most 128 MiB of HBM per device.

```python
import math
import jax
import jax.numpy as jnp
import numpy as np
from jax import lax

D = 6144
HEADS = 48
KV_HEADS = 8
HEAD_DIM = 128
TOP = 4
EXPERTS = 16
FF = 10752
FLIGHT = 2
REQ_DEV = 8
TOKENS = 128
GROUP = 8
FF_DEV = 1344
MOST = 4
CACHE_DEV = 128
LMOST = 64
N_POOL = 16


def shared_keys(key):
    return jnp.clip(jax.random.normal(key, (TOKENS, KV_HEADS, HEAD_DIM), jnp.float32), -5.0, 5.0)


def draw_new_entries(key, part):
    base = shared_keys(key)
    key = jax.random.fold_in(key, 11)
    values = jnp.clip(jax.random.normal(key, (TOKENS, KV_HEADS, HEAD_DIM), jnp.float32), -5.0, 5.0)
    return jnp.stack((base, values), 1).reshape(TOKENS, 2, KV_HEADS * HEAD_DIM).astype(jnp.bfloat16)


def draw_cached(key, part):
    key = jax.random.fold_in(key, 12)
    key_keys, key_values = jax.random.split(key)
    keys = jnp.clip(jax.random.normal(key_keys, (N_POOL * CACHE_DEV, KV_HEADS, HEAD_DIM), jnp.float32), -5.0, 5.0)
    values = jnp.clip(jax.random.normal(key_values, (N_POOL * CACHE_DEV, KV_HEADS, HEAD_DIM), jnp.float32), -5.0, 5.0)
    return jnp.stack((keys, values), 1).reshape(N_POOL * CACHE_DEV, 2, KV_HEADS * HEAD_DIM).astype(jnp.bfloat16)


def draw_queries(key, part):
    key = jax.random.fold_in(key, 13)
    values = jnp.clip(jax.random.normal(key, (TOKENS, HEADS, HEAD_DIM), jnp.float32), -5.0, 5.0)
    return values.reshape(TOKENS, HEADS * HEAD_DIM).astype(jnp.bfloat16)


def draw_hidden_state(key, part):
    key = jax.random.fold_in(key, 14)
    key_main = jax.random.fold_in(key, 0)
    values = jnp.clip(jax.random.normal(key_main, (TOKENS, D), jnp.float32), -5.0, 5.0)
    return values.astype(jnp.bfloat16)


def block_scale(stream_key, dims, cuts, low, high):
    def one(position, blocks):
        steps = jax.random.uniform(jax.random.fold_in(jax.random.fold_in(stream_key, 6), position), (blocks,), jnp.float32, low / len(cuts), high / len(cuts))
        return jnp.repeat(jnp.exp(steps), dims[position] // blocks).reshape((-1,) + (1,) * (len(dims) - position - 1))

    factor_of = one(*cuts[0])
    for cut in cuts[1:]:
        factor_of = factor_of * one(*cut)
    return factor_of


def length_profile(amount, total, limit, skew):
    weights = [(1 << 20) // math.isqrt(rank ** skew) + 1 for rank in range(2, amount + 1)]
    spare, given = total - limit - (amount - 1), [1] * (amount - 1)
    while spare > 0:
        movable = [i for i in range(amount - 1) if given[i] < limit]
        pool, budget = sum([weights[i] for i in movable]), spare
        for i in movable:
            addition = min(limit - given[i], max(1, budget * weights[i] // pool), spare)
            given[i] = given[i] + addition
            spare = spare - addition
    return np.array([limit] + given)


def uneven_parts(stream_key, number_of, total, most, lean):
    if number_of == 2:
        one = jax.random.randint(stream_key, (), max(1, total - most), min(most, total - 1) + 1)
        return jnp.stack([one, total - one])
    tallies = jnp.asarray(length_profile(number_of, total, most, lean), jnp.int32)
    couples = (number_of - 1) // 2
    giver, taker = tallies[1:1 + 2 * couples:2], tallies[2:2 + 2 * couples:2]
    slack = jnp.minimum(giver - 1, most - taker)
    moved = jax.random.randint(jax.random.fold_in(stream_key, 1), (couples,), 0, 1 << 20) % (slack + 1)
    tallies = tallies.at[1:1 + 2 * couples:2].set(giver - moved).at[2:2 + 2 * couples:2].set(taker + moved)
    return tallies[jax.random.permutation(jax.random.fold_in(stream_key, 2), number_of)]


def assign_block(stream_key, own, number, rows, amount, top, limit, lean):
    ranking = jax.random.permutation(stream_key, amount)
    crowded, usual = shares(amount, rows * top, limit, lean, True), shares(amount, rows * top, limit, lean, False)
    places = jnp.arange(amount)

    def named(tallies, turn):
        used = int((tallies > 0).sum())
        fixed = max(1, used // 4)
        passed = fixed + (places - fixed + turn * (used - fixed)) % max(1, amount - fixed)
        return jnp.zeros((amount,), jnp.int32).at[ranking[jnp.where(places < fixed, places, passed)]].set(jnp.asarray(tallies, jnp.int32))

    tallies = jnp.where(number % 4 == 0, named(crowded, number // 4), named(usual, number - number // 4 - 1))
    mixed = jax.random.permutation(jax.random.fold_in(own, 3), amount)
    source_of, sink = mixed[0:amount // 2 * 2:2], mixed[1:amount // 2 * 2:2]
    margin = jnp.minimum(tallies[source_of] - 1, limit - tallies[sink]) // 2
    margin = jnp.where((source_of == ranking[0]) | (sink == ranking[0]) | (tallies[sink] == 0), 0, jnp.maximum(margin, 0))
    passed = jax.random.randint(jax.random.fold_in(own, 4), (amount // 2,), 0, 1 << 20) % (margin + 1)
    tallies = tallies.at[source_of].add(-passed).at[sink].add(passed)
    items = jnp.searchsorted(jnp.cumsum(tallies), jnp.arange(rows * top), side="right").astype(jnp.int32)
    grid = items.reshape(top, rows).T
    grid = grid[jax.random.permutation(jax.random.fold_in(own, 1), rows)]
    turn = jax.random.randint(jax.random.fold_in(own, 2), (rows, 1), 0, top)
    return jnp.take_along_axis(grid, (jnp.arange(top)[None, :] + turn) % top, axis=1)


def shares(number_of, total, reach, slope, full):
    weights = [(1 << 20) // math.isqrt(standing ** slope) + 1 for standing in range(1, number_of + 1)]
    largest = reach if full else min(reach, max(-(-total // number_of), total * weights[0] // sum(weights)))
    least = 1 if total - largest >= number_of - 1 else 0
    given, rest = [largest] + [least] * (number_of - 1), total - largest - least * (number_of - 1)
    while rest > 0:
        candidates = [i for i in range(1, number_of) if given[i] < largest] or [i for i in range(1, number_of) if given[i] < reach]
        mass, budget = sum([weights[i] for i in candidates]), rest
        for i in candidates:
            addition = min(reach - given[i], max(1, budget * weights[i] // mass), rest)
            given[i] = given[i] + addition
            rest = rest - addition
    return np.array(given)


def gaussian(stream_key, extent, scale, most, shards=(), held_as=jnp.bfloat16):
    entries = scale * jax.random.normal(stream_key, extent, jnp.float32)
    if shards:
        entries = entries * block_scale(stream_key, extent, shards, -0.22, 0.18)
    return jnp.clip(entries, -most, most).astype(held_as)


def setup_inputs(seed: int = 0, part: int = 0) -> dict:
    seeds = jax.random.split(jax.random.key(seed), 12)
    part_splits = jax.random.split(jax.random.fold_in(seeds[11], part), 12)
    hidden_state = draw_hidden_state(jax.random.fold_in(jax.random.fold_in(seeds[11], part), 71), part)
    queries = draw_queries(jax.random.fold_in(jax.random.fold_in(seeds[11], part), 71), part)
    new_entries = draw_new_entries(jax.random.fold_in(jax.random.fold_in(seeds[11], part), 71), part)
    cached = draw_cached(jax.random.fold_in(jax.random.fold_in(seeds[11], part), 71), part)
    cache_lengths = jax.vmap(lambda own: uneven_parts(own, REQ_DEV, CACHE_DEV, LMOST, 2))(jax.random.split(part_splits[4], N_POOL)).reshape((N_POOL, REQ_DEV)).astype(jnp.int32)
    routes_keys = jax.random.split(jax.random.fold_in(part_splits[5], 1), TOKENS // REQ_DEV)
    routes_turns = jax.random.permutation(jax.random.fold_in(part_splits[5], 3), TOKENS // REQ_DEV)
    routes = jax.vmap(lambda own, number: assign_block(jax.random.fold_in(part_splits[5], 2), own, number, REQ_DEV, EXPERTS, TOP, MOST, 2))(routes_keys, routes_turns).reshape((TOKENS, TOP))
    norm_gain = jnp.clip(1.0 + 0.15 * jax.random.normal(seeds[6], (D,), jnp.float32), 0.25, 1.75)
    router_weight = gaussian(seeds[7], (D, EXPERTS), D ** -0.5, 0.078125)
    expert_gate = gaussian(seeds[8], (N_POOL, D, FF_DEV), D ** -0.5, 0.078125, ((0, 16),))
    expert_up = gaussian(seeds[9], (N_POOL, D, FF_DEV), D ** -0.5, 0.078125, ((0, 16),))
    expert_down = gaussian(seeds[10], (N_POOL, FF_DEV, D), FF ** -0.5, 0.0625, ((0, 16),))
    return dict(hidden_state=hidden_state, queries=queries, new_entries=new_entries, cached=cached, cache_lengths=cache_lengths, routes=routes, norm_gain=norm_gain, router_weight=router_weight, expert_gate=expert_gate, expert_up=expert_up, expert_down=expert_down)


EPSILON = 1e-05

def attend_local(queries, new_entries, cached, lengths):
    requests = queries.shape[0]
    positions = cached.shape[0]
    groups = HEADS // KV_HEADS
    query_heads = queries.astype(jnp.float32).reshape(requests, KV_HEADS, groups, HEAD_DIM)
    cache_keys = cached[:, 0].astype(jnp.float32).reshape(positions, KV_HEADS, HEAD_DIM)
    cache_values = cached[:, 1].astype(jnp.float32).reshape(positions, KV_HEADS, HEAD_DIM)
    own_keys = new_entries[:, 0].astype(jnp.float32).reshape(requests, KV_HEADS, HEAD_DIM)
    own_values = new_entries[:, 1].astype(jnp.float32).reshape(requests, KV_HEADS, HEAD_DIM)
    scale = 1.0 / math.sqrt(HEAD_DIM)
    scores = jnp.einsum('rkgd,pkd->rkgp', query_heads, cache_keys) * scale
    own_score = jnp.einsum('rkgd,rkd->rkg', query_heads, own_keys) * scale
    ends = jnp.cumsum(lengths, dtype=jnp.int32)
    starts = ends - lengths
    spots = jnp.arange(positions, dtype=jnp.int32)
    inside = (spots[None, :] >= starts[:, None]) & (spots[None, :] < ends[:, None])
    masked = jnp.where(inside[:, None, None, :], scores, -jnp.inf)
    peak = jnp.maximum(lax.optimization_barrier(jnp.max(masked, axis=-1)), own_score)
    expos = jnp.exp(masked - peak[..., None])
    own_expo = jnp.exp(own_score - peak)
    total = lax.optimization_barrier(jnp.sum(expos, axis=-1)) + own_expo
    weights = (expos / total[..., None]).astype(jnp.bfloat16)
    own_weight = (own_expo / total).astype(jnp.bfloat16)
    summed = jnp.einsum('rkgp,pkd->rkgd', weights.astype(jnp.float32), cache_values)
    summed = summed + own_weight.astype(jnp.float32)[..., None] * own_values[:, :, None, :]
    return summed.reshape(requests, HEADS * HEAD_DIM).astype(jnp.bfloat16)

def layer_norm(values, gain):
    center = lax.optimization_barrier(jnp.mean(values, axis=-1, keepdims=True))
    centered = values - center
    spread = lax.optimization_barrier(jnp.mean(centered * centered, axis=-1, keepdims=True))
    return (centered * lax.rsqrt(spread + EPSILON) * gain).astype(jnp.bfloat16)

def reference(hidden_state, queries, new_entries, cached, cache_lengths, routes, norm_gain, router_weight, expert_gate, expert_up, expert_down):
    tokens, width = hidden_state.shape
    experts = router_weight.shape[1]
    per_device = lax.map(lambda items: attend_local(items[0], items[1], items[2], items[3]), (queries.reshape(N_POOL, REQ_DEV, HEADS * HEAD_DIM), new_entries.reshape(N_POOL, REQ_DEV, 2, KV_HEADS * HEAD_DIM), cached.reshape(N_POOL, CACHE_DEV, 2, KV_HEADS * HEAD_DIM), cache_lengths))
    attended = per_device.reshape(tokens, width)
    residual_sum = hidden_state.astype(jnp.float32) + attended.astype(jnp.float32)
    normed = layer_norm(residual_sum, norm_gain)
    logits = jnp.dot(normed, router_weight, preferred_element_type=jnp.float32)
    routed = jnp.take_along_axis(logits, routes, axis=1)
    gates = 1.0 / lax.optimization_barrier(jnp.sum(jnp.exp(routed[:, None, :] - routed[:, :, None]), axis=-1))
    chosen = (routes[:, :, None] == jnp.arange(experts, dtype=jnp.int32)[None, None, :]).astype(jnp.int32)
    counts = lax.optimization_barrier(jnp.sum(chosen, axis=1, dtype=jnp.int32)).reshape(N_POOL, REQ_DEV, experts)
    before = (jnp.cumsum(counts, axis=1, dtype=jnp.int32) - counts).reshape(tokens, experts)
    slots = lax.optimization_barrier(jnp.sum(chosen * before[:, None, :], axis=-1, dtype=jnp.int32))
    owners = jnp.broadcast_to((jnp.arange(tokens, dtype=jnp.int32) // REQ_DEV)[:, None], routes.shape)
    buffer = jnp.zeros((FLIGHT, N_POOL, MOST, width), jnp.bfloat16)
    buffer = buffer.at[routes, owners, slots].set(jnp.broadcast_to(normed[:, None, :], (tokens, TOP, width)), mode='drop')
    gate_all = expert_gate.reshape(FLIGHT, GROUP, width, FF_DEV).transpose(0, 2, 1, 3).reshape(FLIGHT, width, GROUP * FF_DEV)
    up_all = expert_up.reshape(FLIGHT, GROUP, width, FF_DEV).transpose(0, 2, 1, 3).reshape(FLIGHT, width, GROUP * FF_DEV)
    down_all = expert_down.reshape(FLIGHT, GROUP * FF_DEV, width)

    def run_expert(items):
        rows = items[0].reshape(N_POOL * MOST, width)
        gate_part = jnp.dot(rows, items[1], preferred_element_type=jnp.float32)
        up_part = jnp.dot(rows, items[2], preferred_element_type=jnp.float32)
        inner = (jax.nn.silu(gate_part) * up_part).astype(jnp.bfloat16)
        result = jnp.dot(inner, items[3], preferred_element_type=jnp.float32)
        return result.astype(jnp.bfloat16).reshape(N_POOL, MOST, width)
    outputs = lax.map(run_expert, (buffer, gate_all, up_all, down_all))
    held = routes < FLIGHT
    picked = outputs[jnp.minimum(routes, FLIGHT - 1), owners, slots].astype(jnp.float32)
    terms = jnp.where(held[:, :, None], gates[:, :, None] * picked, jnp.float32(0.0))
    mixed = residual_sum + lax.optimization_barrier(jnp.sum(terms, axis=1))
    return mixed.astype(jnp.bfloat16)
```

```python
import functools
import math

import jax
import jax.numpy as jnp
from jax import lax
from jax.experimental import pallas as pl
from jax.experimental.pallas import tpu as pltpu
from jax.sharding import PartitionSpec as P

HEADS = 48
KV_HEADS = 8
HEAD_DIM = 128
FLIGHT = 2
CORES = 2
EPSILON = 1e-05

F32 = jnp.float32
BF16 = jnp.bfloat16
NT = (((1,), (1,)), ((), ()))
TN = (((0,), (0,)), ((), ()))
MIB = 1 << 20


def whole(space=pltpu.VMEM):
    return pl.BlockSpec(memory_space=space)


def iota(shape, dim):
    return lax.broadcasted_iota(jnp.int32, shape, dim)


def slot_columns(routes, expert):
    rows = routes.shape[0]
    named = jnp.max((routes == expert).astype(F32), axis=1, keepdims=True)
    wide = jnp.broadcast_to(named, (rows, rows))
    row, lane = iota((rows, rows), 0), iota((rows, rows), 1)
    named_lanes = jnp.sum(jnp.where(row == lane, wide, 0.0), axis=0, keepdims=True)
    before_lanes = jnp.sum(jnp.where(row < lane, wide, 0.0), axis=0, keepdims=True)
    before = jnp.sum(jnp.where(lane < row, named_lanes, 0.0), axis=1, keepdims=True)
    return named, before, named_lanes, before_lanes


def front_kernel(half, hidden_ref, queries_ref, kv_ref, own_ref, lengths_ref, routes_ref, gain_ref,
                 residual_ref, normed_ref, near_ref, far_ref, att_ref):
    requests, width = hidden_ref.shape
    groups = HEADS // KV_HEADS
    pairs = kv_ref.shape[0]
    scale = 1.0 / math.sqrt(HEAD_DIM)
    row, lane = iota((requests, requests), 0), iota((requests, requests), 1)
    lengths = jnp.broadcast_to(lengths_ref[...], (requests, requests))
    starts = jnp.sum(jnp.where(lane < row, lengths, 0), axis=1, keepdims=True)
    ends = starts + jnp.sum(jnp.where(lane == row, lengths, 0), axis=1, keepdims=True)
    column = iota((requests, pairs), 1)
    inside = (column >= 2 * starts) & (column < 2 * ends) & (column % 2 == 0)
    bias = jnp.where(inside, 0.0, -jnp.inf).astype(F32)
    bias = jnp.concatenate([bias] * groups, axis=0)
    queries = queries_ref[...].astype(F32)
    own = own_ref[...].astype(F32)
    for head in range(KV_HEADS):
        spot = slice(head * HEAD_DIM, (head + 1) * HEAD_DIM)
        block = kv_ref[:, spot]
        own_key, own_value = own[:, 0, spot], own[:, 1, spot]
        parts = [queries[:, (head * groups + j) * HEAD_DIM:(head * groups + j + 1) * HEAD_DIM] for j in range(groups)]
        stacked = jnp.concatenate(parts, axis=0)
        keys = jnp.concatenate([own_key] * groups, axis=0)
        scores = lax.dot_general(stacked.astype(BF16), block, NT, preferred_element_type=F32) * scale + bias
        own_score = jnp.sum(stacked * keys, axis=1, keepdims=True) * scale
        peak = jnp.maximum(jnp.max(scores, axis=1, keepdims=True), own_score)
        expos = jnp.exp(scores - peak)
        own_expo = jnp.exp(own_score - peak)
        total = jnp.sum(expos, axis=1, keepdims=True) + own_expo
        weights = pltpu.roll(expos / total, 1, 1).astype(BF16)
        own_weight = (own_expo / total).astype(BF16).astype(F32)
        summed = jnp.dot(weights, block, preferred_element_type=F32)
        summed = summed + own_weight * jnp.concatenate([own_value] * groups, axis=0)
        for j in range(groups):
            at = (head * groups + j) * HEAD_DIM
            att_ref[:, at:at + HEAD_DIM] = summed[j * requests:(j + 1) * requests].astype(BF16).astype(F32)
    residual = hidden_ref[...].astype(F32) + att_ref[...]
    residual_ref[...] = residual
    centered = residual - jnp.mean(residual, axis=1, keepdims=True)
    spread = jnp.mean(centered * centered, axis=1, keepdims=True)
    normed = (centered * lax.rsqrt(spread + EPSILON) * gain_ref[...]).astype(BF16)
    normed_ref[...] = normed
    mine = half()
    capacity = near_ref.shape[0]
    slot = iota((capacity, requests), 0).astype(F32)
    for expert, out in ((mine, near_ref), (1 - mine, far_ref)):
        _, _, named, before = slot_columns(routes_ref[...], expert)
        placing = jnp.where(before == slot, named, 0.0).astype(BF16)
        out[...] = jnp.dot(placing, normed, preferred_element_type=F32).astype(BF16)


def gate_kernel(half, normed_ref, router_ref, routes_ref, mix_ref):
    routes = routes_ref[...]
    requests, fanout = routes.shape
    experts = router_ref.shape[1]
    capacity = mix_ref.shape[1] // FLIGHT
    logits = jnp.dot(normed_ref[...], router_ref[...], preferred_element_type=F32)
    lane = iota((requests, experts), 1)
    routed = [
        jnp.sum(jnp.where(lane == routes[:, k:k + 1], logits, 0.0), axis=1, keepdims=True) for k in range(fanout)
    ]
    mine = half()
    column = iota((requests, FLIGHT * capacity), 1)
    mix = jnp.zeros((requests, FLIGHT * capacity), F32)
    for turn, expert in enumerate((mine, 1 - mine)):
        named, before, _, _ = slot_columns(routes, expert)
        gate = jnp.zeros((requests, 1), F32)
        for k in range(fanout):
            total = sum(jnp.exp(routed[j] - routed[k]) for j in range(fanout))
            gate = jnp.where(routes[:, k:k + 1] == expert, 1.0 / total, gate)
        place = (column - turn * capacity).astype(F32)
        mix = jnp.where((before == place) & (named > 0.0), gate, mix)
    mix_ref[...] = mix


def expert_kernel(chips, chunk, *refs):
    pieces = refs[:2 * chips]
    gate_hbm, up_hbm, down_hbm, keep_ref, send_ref, rows_ref, gate_ref, up_ref, down_ref, inner_ref, sems = refs[2 * chips:]
    hidden, width = gate_ref.shape
    steps = hidden // chunk

    pairs = ((gate_hbm, gate_ref), (up_hbm, up_ref), (down_hbm, down_ref))

    def copy(i, n):
        at = pl.ds(i * chunk, chunk)
        return pltpu.make_async_copy(pairs[n][0].at[at], pairs[n][1].at[at], sems.at[i, n])

    for i in range(steps):
        copy(i, 0).start()
        copy(i, 1).start()
    for i in range(steps):
        copy(i, 2).start()
    count = pieces[0].shape[0]
    for i, piece in enumerate(pieces):
        rows_ref[i * count:(i + 1) * count, :] = piece[...]
    for i in range(steps):
        at = slice(i * chunk, (i + 1) * chunk)
        copy(i, 0).wait()
        copy(i, 1).wait()
        rows = rows_ref[...]
        gate_part = lax.dot_general(gate_ref[at], rows, NT, preferred_element_type=F32)
        up_part = lax.dot_general(up_ref[at], rows, NT, preferred_element_type=F32)
        inner = gate_part / (1.0 + jnp.exp(-gate_part)) * up_part
        inner_ref[:, at] = inner.T.astype(BF16)
    for i in range(steps):
        copy(i, 2).wait()
    out = jnp.dot(inner_ref[...], down_ref[...], preferred_element_type=F32)
    keep_ref[...] = out[:chips * count]
    send_ref[...] = out[chips * count:].astype(BF16)


def core_sum_kernel(keep_ref, recv_ref, first_ref, *rest):
    count = first_ref.shape[0]
    total = keep_ref[...] + recv_ref[...].astype(F32)
    first_ref[...] = total[:count]
    for i, out in enumerate(rest):
        out[...] = total[(i + 1) * count:(i + 2) * count].astype(BF16)


def chip_sum_kernel(first_ref, *refs):
    *parts, near_ref, far_ref = refs
    total = first_ref[...]
    for part in parts:
        total = total + part[...].astype(F32)
    capacity = near_ref.shape[0]
    near_ref[...] = total[:capacity].astype(BF16)
    far_ref[...] = total[capacity:].astype(BF16)


def mix_kernel(residual_ref, mix_ref, near_ref, far_ref, out_ref):
    mix = mix_ref[...]
    capacity = near_ref.shape[0]
    total = jnp.zeros(residual_ref.shape, F32)
    for i, ref in enumerate((near_ref, far_ref)):
        rows = ref[...].astype(F32)
        for j in range(capacity):
            at = i * capacity + j
            total = total + mix[:, at:at + 1] * rows[j:j + 1]
    out_ref[...] = (residual_ref[...] + total).astype(BF16)


def like(*shape, dtype=BF16):
    return jax.ShapeDtypeStruct(shape, dtype)


def params(mib=16):
    return pltpu.CompilerParams(vmem_limit_bytes=mib * MIB)


def body(
    hidden_state,
    queries,
    new_entries,
    cached,
    cache_lengths,
    routes,
    norm_gain,
    router_weight,
    expert_gate,
    expert_up,
    expert_down,
):
    requests, width = hidden_state.shape
    devices = lax.axis_size("pool")
    group = devices // FLIGHT
    chips = group // CORES
    experts = router_weight.shape[1]
    fanout = routes.shape[1]
    capacity = min(requests, 2 * requests * fanout // experts)
    count = 2 * capacity
    hidden = expert_gate.shape[2]

    def half():
        return lax.axis_index("pool") // group

    def exchange(value, bit):
        return lax.ppermute(value, "pool", [(i, i ^ bit) for i in range(devices)])

    positions = cached.shape[0]
    residual, normed, near, far = pl.pallas_call(
        functools.partial(front_kernel, half),
        out_shape=(like(requests, width, dtype=F32), like(requests, width), like(capacity, width), like(capacity, width)),
        in_specs=[whole()] * 7,
        out_specs=(whole(),) * 4,
        scratch_shapes=[pltpu.VMEM((requests, width), F32)],
        compiler_params=params(),
    )(hidden_state, queries, cached.reshape(2 * positions, -1), new_entries, cache_lengths, routes, norm_gain[None])
    arrived = exchange(far, group)
    mix = pl.pallas_call(
        functools.partial(gate_kernel, half),
        out_shape=like(requests, count, dtype=F32),
        in_specs=[whole()] * 3,
        out_specs=whole(),
        compiler_params=params(),
    )(normed, router_weight, routes)
    own = jnp.concatenate([near, arrived], axis=0)
    mine = [own] + [exchange(own, CORES * j) for j in range(1, chips)]
    beside = [exchange(piece, 1) for piece in mine]
    chunk = hidden // 6 if hidden % 96 == 0 else hidden
    steps = hidden // chunk
    keep, send = pl.pallas_call(
        functools.partial(expert_kernel, chips, chunk),
        out_shape=(like(chips * count, width, dtype=F32), like(chips * count, width)),
        in_specs=[whole()] * (2 * chips) + [whole(pl.ANY)] * 3,
        out_specs=(whole(), whole()),
        scratch_shapes=[
            pltpu.VMEM((2 * chips * count, width), BF16),
            pltpu.VMEM((hidden, width), BF16),
            pltpu.VMEM((hidden, width), BF16),
            pltpu.VMEM((hidden, width), BF16),
            pltpu.VMEM((2 * chips * count, hidden), BF16),
            pltpu.SemaphoreType.DMA((steps, 3)),
        ],
        compiler_params=params(60),
    )(*mine, *beside, jnp.swapaxes(expert_gate, 1, 2)[0], jnp.swapaxes(expert_up, 1, 2)[0], expert_down[0])
    recv = exchange(send, 1)
    first, *rest = pl.pallas_call(
        core_sum_kernel,
        out_shape=(like(count, width, dtype=F32),) + (like(count, width),) * (chips - 1),
        in_specs=[whole()] * 2,
        out_specs=(whole(),) * chips,
        compiler_params=params(32),
    )(keep, recv)
    parts = [exchange(piece, CORES * (j + 1)) for j, piece in enumerate(rest)]
    near_out, far_out = pl.pallas_call(
        chip_sum_kernel,
        out_shape=(like(capacity, width), like(capacity, width)),
        in_specs=[whole()] * chips,
        out_specs=(whole(), whole()),
        compiler_params=params(),
    )(first, *parts)
    back = exchange(far_out, group)
    return pl.pallas_call(
        mix_kernel,
        out_shape=like(requests, width),
        in_specs=[whole()] * 4,
        out_specs=whole(),
        compiler_params=params(),
    )(residual, mix, near_out, back)


def solution(mesh):
    in_specs = (
        P(("rep", "pool"), None),
        P(("rep", "pool"), None),
        P(("rep", "pool"), None, None),
        P(("rep", "pool"), None, None),
        P(("rep", "pool"), None),
        P(("rep", "pool"), None),
        P(),
        P(),
        P("pool", None, None),
        P("pool", None, None),
        P("pool", None, None),
    )
    out_specs = P(("rep", "pool"), None)
    return jax.shard_map(body, mesh=mesh, in_specs=in_specs, out_specs=out_specs, check_vma=False)
```

```python
import functools
import math

import jax
import jax.numpy as jnp
from jax import lax
from jax.experimental import pallas as pl
from jax.experimental.pallas import tpu as pltpu
from jax.sharding import PartitionSpec as P

HEADS = 48
KV_HEADS = 8
HEAD_DIM = 128
FLIGHT = 2
CORES = 2
EPSILON = 1e-05

F32 = jnp.float32
BF16 = jnp.bfloat16
NT = (((1,), (1,)), ((), ()))
TN = (((0,), (0,)), ((), ()))
MIB = 1 << 20


def whole(space=pltpu.VMEM):
    return pl.BlockSpec(memory_space=space)


def iota(shape, dim):
    return lax.broadcasted_iota(jnp.int32, shape, dim)


def spread(rows):
    n = rows.shape[1]
    return jnp.broadcast_to(rows, (n, n)), iota((n, n), 0), iota((n, n), 1)


def to_column(values):
    wide, row, lane = spread(values)
    return jnp.sum(jnp.where(row == lane, wide, 0.0), axis=1, keepdims=True)


def slot_rows(routes, expert):
    named = jnp.max((routes == expert).astype(F32), axis=0, keepdims=True)
    column = to_column(named)
    _, row, lane = spread(named)
    before = jnp.sum(jnp.where(row < lane, column, 0.0), axis=0, keepdims=True)
    return named, before


def front_kernel(half, hidden_hbm, queries_hbm, cached_hbm, own_hbm, lengths_hbm, routes_hbm, gain_hbm,
                 residual_ref, normed_ref, near_ref, far_ref,
                 hidden_ref, queries_ref, kv_ref, own_ref, lengths_ref, routes_ref, gain_ref, wide_ref, att_ref, sems):
    pairs = (
        (lengths_hbm, lengths_ref),
        (queries_hbm, queries_ref),
        (cached_hbm.reshape(kv_ref.shape), kv_ref),
        (own_hbm.reshape(own_ref.shape), own_ref),
        (hidden_hbm, hidden_ref),
        (gain_hbm, gain_ref),
        (routes_hbm, routes_ref),
    )
    copies = [pltpu.make_async_copy(src, dst, sems.at[i]) for i, (src, dst) in enumerate(pairs)]
    for copy in copies:
        copy.start()
    requests, width = hidden_ref.shape
    groups = HEADS // KV_HEADS
    positions = kv_ref.shape[0]
    scale = 1.0 / math.sqrt(HEAD_DIM)
    row, lane = iota((requests, requests), 0), iota((requests, requests), 1)
    copies[0].wait()
    lengths = jnp.broadcast_to(lengths_ref[...], (requests, requests))
    starts = jnp.sum(jnp.where(lane < row, lengths, 0), axis=1, keepdims=True)
    ends = starts + jnp.sum(jnp.where(lane == row, lengths, 0), axis=1, keepdims=True)
    column = iota((requests, positions), 1)
    inside = (column >= 2 * starts) & (column < 2 * ends) & (column % 2 == 0)
    bias = jnp.where(inside, 0.0, -jnp.inf).astype(F32)
    bias = jnp.concatenate([bias] * groups, axis=0)
    copies[1].wait()
    queries = queries_ref[...].astype(F32)
    copies[3].wait()
    for head in range(KV_HEADS):
        wide_ref[head] = own_ref[:, head * HEAD_DIM:(head + 1) * HEAD_DIM].astype(F32)
    copies[2].wait()
    for head in range(KV_HEADS):
        spot = slice(head * HEAD_DIM, (head + 1) * HEAD_DIM)
        block = kv_ref[:, spot]
        parts = [queries[:, (head * groups + j) * HEAD_DIM:(head * groups + j + 1) * HEAD_DIM] for j in range(groups)]
        stacked = jnp.concatenate(parts, axis=0)
        keys = jnp.concatenate([wide_ref[head, pl.ds(0, requests, stride=2), :]] * groups, axis=0)
        scores = lax.dot_general(stacked.astype(BF16), block, NT, preferred_element_type=F32) * scale + bias
        own_score = jnp.sum(stacked * keys, axis=1, keepdims=True) * scale
        peak = jnp.maximum(jnp.max(scores, axis=1, keepdims=True), own_score)
        expos = jnp.exp(scores - peak)
        own_expo = jnp.exp(own_score - peak)
        total = jnp.sum(expos, axis=1, keepdims=True) + own_expo
        weights = pltpu.roll(expos / total, 1, 1).astype(BF16)
        own_weight = (own_expo / total).astype(BF16).astype(F32)
        summed = jnp.dot(weights, block, preferred_element_type=F32)
        summed = summed + own_weight * jnp.concatenate([wide_ref[head, pl.ds(1, requests, stride=2), :]] * groups, axis=0)
        for j in range(groups):
            at = (head * groups + j) * HEAD_DIM
            att_ref[:, at:at + HEAD_DIM] = summed[j * requests:(j + 1) * requests].astype(BF16).astype(F32)
    copies[4].wait()
    residual = hidden_ref[...].astype(F32) + att_ref[...]
    residual_ref[...] = residual
    centered = residual - jnp.mean(residual, axis=1, keepdims=True)
    spread_of = jnp.mean(centered * centered, axis=1, keepdims=True)
    copies[5].wait()
    normed = (centered * lax.rsqrt(spread_of + EPSILON) * gain_ref[...]).astype(BF16)
    normed_ref[...] = normed
    copies[6].wait()
    mine = half()
    capacity = near_ref.shape[0]
    slot = iota((capacity, requests), 0).astype(F32)
    for expert, out in ((mine, near_ref), (1 - mine, far_ref)):
        named, before = slot_rows(routes_ref[...], expert)
        placing = jnp.where(before == slot, named, 0.0).astype(BF16)
        out[...] = jnp.dot(placing, normed, preferred_element_type=F32).astype(BF16)


def gate_kernel(half, normed_ref, router_ref, routes_ref, mix_ref):
    routes = routes_ref[...]
    fanout, requests = routes.shape
    experts = router_ref.shape[0]
    capacity = mix_ref.shape[1] // FLIGHT
    logits = lax.dot_general(normed_ref[...], router_ref[...], NT, preferred_element_type=F32)
    lane = iota((requests, experts), 1).astype(F32)
    columns = [to_column(routes[k:k + 1].astype(F32)) for k in range(fanout)]
    routed = [jnp.sum(jnp.where(lane == columns[k], logits, 0.0), axis=1, keepdims=True) for k in range(fanout)]
    gates = [1.0 / sum(jnp.exp(routed[j] - routed[k]) for j in range(fanout)) for k in range(fanout)]
    mine = half()
    column = iota((requests, FLIGHT * capacity), 1)
    mix = jnp.zeros((requests, FLIGHT * capacity), F32)
    for turn, expert in enumerate((mine, 1 - mine)):
        named, before = slot_rows(routes, expert)
        named, before = to_column(named), to_column(before)
        gate = jnp.zeros((requests, 1), F32)
        for k in range(fanout):
            gate = jnp.where(columns[k] == expert.astype(F32), gates[k], gate)
        place = (column - turn * capacity).astype(F32)
        mix = jnp.where((before == place) & (named > 0.0), gate, mix)
    mix_ref[...] = mix


def join_kernel(near_ref, arrived_ref, out_ref):
    out_ref[...] = jnp.concatenate([near_ref[...], arrived_ref[...]], axis=0)


def expert_kernel(chips, chunk, *refs):
    pieces = refs[:2 * chips]
    gate_ref, up_ref, down_ref, keep_ref, send_ref, rows_ref, inner_ref = refs[2 * chips:]
    hidden, width = gate_ref.shape
    steps = hidden // chunk
    count = pieces[0].shape[0]
    for i, piece in enumerate(pieces):
        rows_ref[i * count:(i + 1) * count, :] = piece[...]
    for i in range(steps):
        at = slice(i * chunk, (i + 1) * chunk)
        rows = rows_ref[...]
        gate_part = lax.dot_general(gate_ref[at], rows, NT, preferred_element_type=F32)
        up_part = lax.dot_general(up_ref[at], rows, NT, preferred_element_type=F32)
        inner = gate_part / (1.0 + jnp.exp(-gate_part)) * up_part
        inner_ref[:, at] = inner.T.astype(BF16)
    part = width // 8 if width % 1024 == 0 else width
    for i in range(width // part):
        at = slice(i * part, (i + 1) * part)
        out = jnp.dot(inner_ref[...], down_ref[:, at], preferred_element_type=F32)
        keep_ref[:, at] = out[:chips * count]
        send_ref[:, at] = out[chips * count:].astype(BF16)


def core_sum_kernel(keep_ref, recv_ref, first_ref, *rest):
    count = first_ref.shape[0]
    total = keep_ref[...] + recv_ref[...].astype(F32)
    first_ref[...] = total[:count]
    for i, out in enumerate(rest):
        out[...] = total[(i + 1) * count:(i + 2) * count].astype(BF16)


def chip_sum_kernel(first_ref, *refs):
    *parts, near_ref, far_ref = refs
    total = first_ref[...]
    for part in parts:
        total = total + part[...].astype(F32)
    capacity = near_ref.shape[0]
    near_ref[...] = total[:capacity].astype(BF16)
    far_ref[...] = total[capacity:].astype(BF16)


def mix_kernel(residual_ref, mix_ref, near_ref, far_ref, out_ref):
    mix = mix_ref[...]
    capacity = near_ref.shape[0]
    total = jnp.zeros(residual_ref.shape, F32)
    for i, ref in enumerate((near_ref, far_ref)):
        rows = ref[...].astype(F32)
        for j in range(capacity):
            at = i * capacity + j
            total = total + mix[:, at:at + 1] * rows[j:j + 1]
    out_ref[...] = (residual_ref[...] + total).astype(BF16)


def like(*shape, dtype=BF16):
    return jax.ShapeDtypeStruct(shape, dtype)


def params(mib):
    return pltpu.CompilerParams(vmem_limit_bytes=mib * MIB)


def body(
    hidden_state,
    queries,
    new_entries,
    cached,
    cache_lengths,
    routes,
    norm_gain,
    router_weight,
    expert_gate,
    expert_up,
    expert_down,
):
    requests, width = hidden_state.shape
    devices = lax.axis_size("pool")
    group = devices // FLIGHT
    chips = group // CORES
    experts = router_weight.shape[1]
    fanout = routes.shape[1]
    capacity = min(requests, 2 * requests * fanout // experts)
    count = 2 * capacity
    hidden = expert_gate.shape[2]

    tight = 6 * hidden * width > 24 * MIB

    def half():
        return lax.axis_index("pool") // group

    def exchange(value, bit):
        return lax.ppermute(value, "pool", [(i, i ^ bit) for i in range(devices)])

    positions = cached.shape[0]
    heads = cached.shape[2]
    weights = [
        pltpu.with_memory_space_constraint(w, pltpu.VMEM)
        for w in (jnp.swapaxes(expert_gate, 1, 2)[0], jnp.swapaxes(expert_up, 1, 2)[0], expert_down[0])
    ]
    routes = routes.T
    front = (hidden_state, queries, cached, new_entries, cache_lengths, routes, norm_gain[None])
    residual, normed, near, far = pl.pallas_call(
        functools.partial(front_kernel, half),
        out_shape=(like(requests, width, dtype=F32), like(requests, width), like(capacity, width), like(capacity, width)),
        in_specs=[whole(pltpu.HBM)] * 7,
        out_specs=(whole(),) * 4,
        scratch_shapes=[
            pltpu.VMEM((requests, width), BF16),
            pltpu.VMEM((requests, width), BF16),
            pltpu.VMEM((2 * positions, heads), BF16),
            pltpu.VMEM((2 * requests, heads), BF16),
            pltpu.VMEM((1, requests), jnp.int32),
            pltpu.VMEM((fanout, requests), jnp.int32),
            pltpu.VMEM((1, width), F32),
            pltpu.VMEM((KV_HEADS, 2 * requests, HEAD_DIM), F32),
            pltpu.VMEM((requests, width), F32),
            pltpu.SemaphoreType.DMA((7,)),
        ],
        compiler_params=params(2 if tight else 24),
        cost_estimate=pl.CostEstimate(flops=200_000_000_000, bytes_accessed=50_000_000, transcendentals=0),
    )(*(pltpu.with_memory_space_constraint(x, pltpu.HBM) for x in front))
    arrived = exchange(far, group)
    mix = pl.pallas_call(
        functools.partial(gate_kernel, half),
        out_shape=like(requests, count, dtype=F32),
        in_specs=[whole()] * 3,
        out_specs=whole(),
        compiler_params=params(2 if tight else 24),
    )(normed, router_weight.T, routes)
    own = pl.pallas_call(
        join_kernel,
        out_shape=like(count, width),
        in_specs=[whole()] * 2,
        out_specs=whole(),
        compiler_params=params(2 if tight else 24),
    )(near, arrived)
    mine = [own] + [exchange(own, CORES * j) for j in range(1, chips)]
    beside = [exchange(piece, 1) for piece in mine]
    chunk = hidden // 6 if hidden % 96 == 0 else hidden
    steps = hidden // chunk
    keep, send = pl.pallas_call(
        functools.partial(expert_kernel, chips, chunk),
        out_shape=(like(chips * count, width, dtype=F32), like(chips * count, width)),
        in_specs=[whole()] * (2 * chips + 3),
        out_specs=(whole(), whole()),
        scratch_shapes=[
            pltpu.VMEM((2 * chips * count, width), BF16),
            pltpu.VMEM((2 * chips * count, hidden), BF16),
        ],
        compiler_params=params(3 if tight else 24),
    )(*mine, *beside, *weights)
    recv = exchange(send, 1)
    first, *rest = pl.pallas_call(
        core_sum_kernel,
        out_shape=(like(count, width, dtype=F32),) + (like(count, width),) * (chips - 1),
        in_specs=[whole()] * 2,
        out_specs=(whole(),) * chips,
        compiler_params=params(2 if tight else 24),
    )(pltpu.with_memory_space_constraint(keep, pltpu.VMEM), recv)
    parts = [exchange(piece, CORES * (j + 1)) for j, piece in enumerate(rest)]
    near_out, far_out = pl.pallas_call(
        chip_sum_kernel,
        out_shape=(like(capacity, width), like(capacity, width)),
        in_specs=[whole()] * chips,
        out_specs=(whole(), whole()),
        compiler_params=params(2 if tight else 24),
    )(first, *parts)
    back = exchange(far_out, group)
    return pl.pallas_call(
        mix_kernel,
        out_shape=like(requests, width),
        in_specs=[whole()] * 4,
        out_specs=whole(),
        compiler_params=params(2 if tight else 24),
    )(residual, mix, near_out, back)


def solution(mesh):
    in_specs = (
        P(("rep", "pool"), None),
        P(("rep", "pool"), None),
        P(("rep", "pool"), None, None),
        P(("rep", "pool"), None, None),
        P(("rep", "pool"), None),
        P(("rep", "pool"), None),
        P(),
        P(),
        P("pool", None, None),
        P("pool", None, None),
        P("pool", None, None),
    )
    out_specs = P(("rep", "pool"), None)
    return jax.shard_map(body, mesh=mesh, in_specs=in_specs, out_specs=out_specs, check_vma=False)
```

```python
import functools
import math

import jax
import jax.numpy as jnp
from jax import lax
from jax.experimental import pallas as pl
from jax.experimental.pallas import tpu as pltpu
from jax.sharding import PartitionSpec as P

HEADS = 48
KV_HEADS = 8
HEAD_DIM = 128
FLIGHT = 2
CORES = 2
EPSILON = 1e-05

F32 = jnp.float32
BF16 = jnp.bfloat16
NT = (((1,), (1,)), ((), ()))
TN = (((0,), (0,)), ((), ()))
MIB = 1 << 20


def whole(space=pltpu.VMEM):
    return pl.BlockSpec(memory_space=space)


def iota(shape, dim):
    return lax.broadcasted_iota(jnp.int32, shape, dim)


def spread(rows):
    n = rows.shape[1]
    return jnp.broadcast_to(rows, (n, n)), iota((n, n), 0), iota((n, n), 1)


def to_column(values):
    wide, row, lane = spread(values)
    return jnp.sum(jnp.where(row == lane, wide, 0.0), axis=1, keepdims=True)


def slot_rows(routes, expert):
    named = jnp.max((routes == expert).astype(F32), axis=0, keepdims=True)
    column = to_column(named)
    _, row, lane = spread(named)
    before = jnp.sum(jnp.where(row < lane, column, 0.0), axis=0, keepdims=True)
    return named, before


def front_kernel(half, hidden_hbm, queries_hbm, cached_hbm, own_hbm, lengths_hbm, routes_hbm, gain_hbm,
                 residual_ref, normed_ref, near_ref, far_ref,
                 hidden_ref, queries_ref, kv_ref, own_ref, lengths_ref, routes_ref, gain_ref, wide_ref, att_ref, sems):
    pairs = (
        (lengths_hbm, lengths_ref),
        (queries_hbm, queries_ref),
        (cached_hbm.reshape(kv_ref.shape), kv_ref),
        (own_hbm.reshape(own_ref.shape), own_ref),
        (hidden_hbm, hidden_ref),
        (gain_hbm, gain_ref),
        (routes_hbm, routes_ref),
    )
    copies = [pltpu.make_async_copy(src, dst, sems.at[i]) for i, (src, dst) in enumerate(pairs)]
    for copy in copies:
        copy.start()
    requests, width = hidden_ref.shape
    groups = HEADS // KV_HEADS
    positions = kv_ref.shape[0]
    scale = 1.0 / math.sqrt(HEAD_DIM)
    row, lane = iota((requests, requests), 0), iota((requests, requests), 1)
    copies[0].wait()
    lengths = jnp.broadcast_to(lengths_ref[...], (requests, requests))
    starts = jnp.sum(jnp.where(lane < row, lengths, 0), axis=1, keepdims=True)
    ends = starts + jnp.sum(jnp.where(lane == row, lengths, 0), axis=1, keepdims=True)
    column = iota((requests, positions), 1)
    inside = (column >= 2 * starts) & (column < 2 * ends) & (column % 2 == 0)
    bias = jnp.where(inside, 0.0, -jnp.inf).astype(F32)
    bias = jnp.concatenate([bias] * groups, axis=0)
    copies[1].wait()
    queries = queries_ref[...].astype(F32)
    copies[3].wait()
    for head in range(KV_HEADS):
        wide_ref[head] = own_ref[:, head * HEAD_DIM:(head + 1) * HEAD_DIM].astype(F32)
    copies[2].wait()
    heads = range(KV_HEADS)
    blocks = [kv_ref[:, head * HEAD_DIM:(head + 1) * HEAD_DIM] for head in heads]
    stacks = []
    for head in heads:
        at = head * groups * HEAD_DIM
        stacks.append(jnp.concatenate([queries[:, at + j * HEAD_DIM:at + (j + 1) * HEAD_DIM] for j in range(groups)], axis=0))
    keys = [jnp.concatenate([wide_ref[head, pl.ds(0, requests, stride=2), :]] * groups, axis=0) for head in heads]
    raw = [lax.dot_general(s.astype(BF16), k, NT, preferred_element_type=F32) for s, k in zip(stacks, blocks)]
    own_scores = [jnp.sum(s * k, axis=1, keepdims=True) * scale for s, k in zip(stacks, keys)]
    weights, own_weights = [], []
    for r, own_score in zip(raw, own_scores):
        scores = r * scale + bias
        peak = jnp.maximum(jnp.max(scores, axis=1, keepdims=True), own_score)
        expos = jnp.exp(scores - peak)
        own_expo = jnp.exp(own_score - peak)
        total = jnp.sum(expos, axis=1, keepdims=True) + own_expo
        weights.append(pltpu.roll(expos / total, 1, 1).astype(BF16))
        own_weights.append((own_expo / total).astype(BF16).astype(F32))
    sums = [jnp.dot(w, k, preferred_element_type=F32) for w, k in zip(weights, blocks)]
    for head, summed, own_weight in zip(heads, sums, own_weights):
        summed = summed + own_weight * jnp.concatenate([wide_ref[head, pl.ds(1, requests, stride=2), :]] * groups, axis=0)
        for j in range(groups):
            at = (head * groups + j) * HEAD_DIM
            att_ref[:, at:at + HEAD_DIM] = summed[j * requests:(j + 1) * requests].astype(BF16).astype(F32)
    copies[4].wait()
    residual = hidden_ref[...].astype(F32) + att_ref[...]
    residual_ref[...] = residual
    centered = residual - jnp.mean(residual, axis=1, keepdims=True)
    spread_of = jnp.mean(centered * centered, axis=1, keepdims=True)
    copies[5].wait()
    normed = (centered * lax.rsqrt(spread_of + EPSILON) * gain_ref[...]).astype(BF16)
    normed_ref[...] = normed
    copies[6].wait()
    mine = half()
    capacity = near_ref.shape[0]
    slot = iota((capacity, requests), 0).astype(F32)
    for expert, out in ((mine, near_ref), (1 - mine, far_ref)):
        named, before = slot_rows(routes_ref[...], expert)
        placing = jnp.where(before == slot, named, 0.0).astype(BF16)
        out[...] = jnp.dot(placing, normed, preferred_element_type=F32).astype(BF16)


def gate_kernel(half, normed_ref, router_ref, routes_ref, mix_ref):
    routes = routes_ref[...]
    fanout, requests = routes.shape
    experts = router_ref.shape[0]
    capacity = mix_ref.shape[1] // FLIGHT
    logits = lax.dot_general(normed_ref[...], router_ref[...], NT, preferred_element_type=F32)
    lane = iota((requests, experts), 1).astype(F32)
    columns = [to_column(routes[k:k + 1].astype(F32)) for k in range(fanout)]
    routed = [jnp.sum(jnp.where(lane == columns[k], logits, 0.0), axis=1, keepdims=True) for k in range(fanout)]
    gates = [1.0 / sum(jnp.exp(routed[j] - routed[k]) for j in range(fanout)) for k in range(fanout)]
    mine = half()
    column = iota((requests, FLIGHT * capacity), 1)
    mix = jnp.zeros((requests, FLIGHT * capacity), F32)
    for turn, expert in enumerate((mine, 1 - mine)):
        named, before = slot_rows(routes, expert)
        named, before = to_column(named), to_column(before)
        gate = jnp.zeros((requests, 1), F32)
        for k in range(fanout):
            gate = jnp.where(columns[k] == expert.astype(F32), gates[k], gate)
        place = (column - turn * capacity).astype(F32)
        mix = jnp.where((before == place) & (named > 0.0), gate, mix)
    mix_ref[...] = mix


def join_kernel(near_ref, arrived_ref, out_ref):
    out_ref[...] = jnp.concatenate([near_ref[...], arrived_ref[...]], axis=0)


def expert_kernel(chips, chunk, *refs):
    pieces = refs[:2 * chips]
    gate_ref, up_ref, down_ref, keep_ref, send_ref, rows_ref, inner_ref = refs[2 * chips:]
    hidden, width = gate_ref.shape
    steps = hidden // chunk
    count = pieces[0].shape[0]
    for i, piece in enumerate(pieces):
        rows_ref[i * count:(i + 1) * count, :] = piece[...]
    for i in range(steps):
        at = slice(i * chunk, (i + 1) * chunk)
        rows = rows_ref[...]
        gate_part = lax.dot_general(gate_ref[at], rows, NT, preferred_element_type=F32)
        up_part = lax.dot_general(up_ref[at], rows, NT, preferred_element_type=F32)
        inner = gate_part / (1.0 + jnp.exp(-gate_part)) * up_part
        inner_ref[:, at] = inner.T.astype(BF16)
    part = width // 8 if width % 1024 == 0 else width
    for i in range(width // part):
        at = slice(i * part, (i + 1) * part)
        out = jnp.dot(inner_ref[...], down_ref[:, at], preferred_element_type=F32)
        keep_ref[:, at] = out[:chips * count]
        send_ref[:, at] = out[chips * count:].astype(BF16)


def core_sum_kernel(keep_ref, recv_ref, first_ref, *rest):
    count = first_ref.shape[0]
    total = keep_ref[...] + recv_ref[...].astype(F32)
    first_ref[...] = total[:count]
    for i, out in enumerate(rest):
        out[...] = total[(i + 1) * count:(i + 2) * count].astype(BF16)


def chip_sum_kernel(first_ref, *refs):
    *parts, near_ref, far_ref = refs
    total = first_ref[...]
    for part in parts:
        total = total + part[...].astype(F32)
    capacity = near_ref.shape[0]
    near_ref[...] = total[:capacity].astype(BF16)
    far_ref[...] = total[capacity:].astype(BF16)


def mix_kernel(residual_ref, mix_ref, near_ref, far_ref, out_ref):
    mix = mix_ref[...]
    capacity = near_ref.shape[0]
    total = jnp.zeros(residual_ref.shape, F32)
    for i, ref in enumerate((near_ref, far_ref)):
        rows = ref[...].astype(F32)
        for j in range(capacity):
            at = i * capacity + j
            total = total + mix[:, at:at + 1] * rows[j:j + 1]
    out_ref[...] = (residual_ref[...] + total).astype(BF16)


def like(*shape, dtype=BF16):
    return jax.ShapeDtypeStruct(shape, dtype)


def params(mib):
    return pltpu.CompilerParams(vmem_limit_bytes=mib * MIB)


def body(
    hidden_state,
    queries,
    new_entries,
    cached,
    cache_lengths,
    routes,
    norm_gain,
    router_weight,
    expert_gate,
    expert_up,
    expert_down,
):
    requests, width = hidden_state.shape
    devices = lax.axis_size("pool")
    group = devices // FLIGHT
    chips = group // CORES
    experts = router_weight.shape[1]
    fanout = routes.shape[1]
    capacity = min(requests, 2 * requests * fanout // experts)
    count = 2 * capacity
    hidden = expert_gate.shape[2]

    tight = 6 * hidden * width > 24 * MIB

    def half():
        return lax.axis_index("pool") // group

    def exchange(value, bit):
        return lax.ppermute(value, "pool", [(i, i ^ bit) for i in range(devices)])

    positions = cached.shape[0]
    heads = cached.shape[2]
    weights = [
        pltpu.with_memory_space_constraint(w, pltpu.VMEM)
        for w in (jnp.swapaxes(expert_gate, 1, 2)[0], jnp.swapaxes(expert_up, 1, 2)[0], expert_down[0])
    ]
    routes = routes.T
    front = (hidden_state, queries, cached, new_entries, cache_lengths, routes, norm_gain[None])
    residual, normed, near, far = pl.pallas_call(
        functools.partial(front_kernel, half),
        out_shape=(like(requests, width, dtype=F32), like(requests, width), like(capacity, width), like(capacity, width)),
        in_specs=[whole(pltpu.HBM)] * 7,
        out_specs=(whole(),) * 4,
        scratch_shapes=[
            pltpu.VMEM((requests, width), BF16),
            pltpu.VMEM((requests, width), BF16),
            pltpu.VMEM((2 * positions, heads), BF16),
            pltpu.VMEM((2 * requests, heads), BF16),
            pltpu.VMEM((1, requests), jnp.int32),
            pltpu.VMEM((fanout, requests), jnp.int32),
            pltpu.VMEM((1, width), F32),
            pltpu.VMEM((KV_HEADS, 2 * requests, HEAD_DIM), F32),
            pltpu.VMEM((requests, width), F32),
            pltpu.SemaphoreType.DMA((7,)),
        ],
        compiler_params=params(2 if tight else 24),
        cost_estimate=pl.CostEstimate(flops=200_000_000_000, bytes_accessed=50_000_000, transcendentals=0),
    )(*(pltpu.with_memory_space_constraint(x, pltpu.HBM) for x in front))
    arrived = exchange(far, group)
    mix = pl.pallas_call(
        functools.partial(gate_kernel, half),
        out_shape=like(requests, count, dtype=F32),
        in_specs=[whole()] * 3,
        out_specs=whole(),
        compiler_params=params(2 if tight else 24),
    )(normed, router_weight.T, routes)
    own = pl.pallas_call(
        join_kernel,
        out_shape=like(count, width),
        in_specs=[whole()] * 2,
        out_specs=whole(),
        compiler_params=params(2 if tight else 24),
    )(near, arrived)
    mine = [own] + [exchange(own, CORES * j) for j in range(1, chips)]
    beside = [exchange(piece, 1) for piece in mine]
    chunk = hidden // 6 if hidden % 96 == 0 else hidden
    steps = hidden // chunk
    keep, send = pl.pallas_call(
        functools.partial(expert_kernel, chips, chunk),
        out_shape=(like(chips * count, width, dtype=F32), like(chips * count, width)),
        in_specs=[whole()] * (2 * chips + 3),
        out_specs=(whole(), whole()),
        scratch_shapes=[
            pltpu.VMEM((2 * chips * count, width), BF16),
            pltpu.VMEM((2 * chips * count, hidden), BF16),
        ],
        compiler_params=params(3 if tight else 24),
    )(*mine, *beside, *weights)
    recv = exchange(send, 1)
    first, *rest = pl.pallas_call(
        core_sum_kernel,
        out_shape=(like(count, width, dtype=F32),) + (like(count, width),) * (chips - 1),
        in_specs=[whole()] * 2,
        out_specs=(whole(),) * chips,
        compiler_params=params(2 if tight else 24),
    )(pltpu.with_memory_space_constraint(keep, pltpu.VMEM), recv)
    parts = [exchange(piece, CORES * (j + 1)) for j, piece in enumerate(rest)]
    near_out, far_out = pl.pallas_call(
        chip_sum_kernel,
        out_shape=(like(capacity, width), like(capacity, width)),
        in_specs=[whole()] * chips,
        out_specs=(whole(), whole()),
        compiler_params=params(2 if tight else 24),
    )(first, *parts)
    back = exchange(far_out, group)
    return pl.pallas_call(
        mix_kernel,
        out_shape=like(requests, width),
        in_specs=[whole()] * 4,
        out_specs=whole(),
        compiler_params=params(2 if tight else 24),
    )(residual, mix, near_out, back)


def solution(mesh):
    in_specs = (
        P(("rep", "pool"), None),
        P(("rep", "pool"), None),
        P(("rep", "pool"), None, None),
        P(("rep", "pool"), None, None),
        P(("rep", "pool"), None),
        P(("rep", "pool"), None),
        P(),
        P(),
        P("pool", None, None),
        P("pool", None, None),
        P("pool", None, None),
    )
    out_specs = P(("rep", "pool"), None)
    return jax.shard_map(body, mesh=mesh, in_specs=in_specs, out_specs=out_specs, check_vma=False)
```

```python
import functools
import math

import jax
import jax.numpy as jnp
from jax import lax
from jax.experimental import pallas as pl
from jax.experimental.pallas import tpu as pltpu
from jax.sharding import PartitionSpec as P

HEADS = 48
KV_HEADS = 8
HEAD_DIM = 128
FLIGHT = 2
CORES = 2
EPSILON = 1e-05

F32 = jnp.float32
BF16 = jnp.bfloat16
NT = (((1,), (1,)), ((), ()))
TN = (((0,), (0,)), ((), ()))
MIB = 1 << 20


def whole(space=pltpu.VMEM):
    return pl.BlockSpec(memory_space=space)


def iota(shape, dim):
    return lax.broadcasted_iota(jnp.int32, shape, dim)


def spread(rows):
    n = rows.shape[1]
    return jnp.broadcast_to(rows, (n, n)), iota((n, n), 0), iota((n, n), 1)


def to_column(values):
    wide, row, lane = spread(values)
    return jnp.sum(jnp.where(row == lane, wide, 0.0), axis=1, keepdims=True)


def slot_rows(routes, expert):
    named = jnp.max((routes == expert).astype(F32), axis=0, keepdims=True)
    column = to_column(named)
    _, row, lane = spread(named)
    before = jnp.sum(jnp.where(row < lane, column, 0.0), axis=0, keepdims=True)
    return named, before


def front_kernel(half, hidden_hbm, queries_hbm, cached_hbm, own_hbm, lengths_hbm, routes_hbm, gain_hbm,
                 residual_ref, normed_ref, near_ref, far_ref,
                 hidden_ref, queries_ref, kv_ref, own_ref, lengths_ref, routes_ref, gain_ref, wide_ref, att_ref, sems):
    pairs = (
        (lengths_hbm, lengths_ref),
        (queries_hbm, queries_ref),
        (cached_hbm.reshape(kv_ref.shape), kv_ref),
        (own_hbm.reshape(own_ref.shape), own_ref),
        (hidden_hbm, hidden_ref),
        (gain_hbm, gain_ref),
        (routes_hbm, routes_ref),
    )
    copies = [pltpu.make_async_copy(src, dst, sems.at[i]) for i, (src, dst) in enumerate(pairs)]
    for copy in copies:
        copy.start()
    requests, width = hidden_ref.shape
    groups = HEADS // KV_HEADS
    positions = kv_ref.shape[0]
    scale = 1.0 / math.sqrt(HEAD_DIM)
    row, lane = iota((requests, requests), 0), iota((requests, requests), 1)
    copies[0].wait()
    lengths = jnp.broadcast_to(lengths_ref[...], (requests, requests))
    starts = jnp.sum(jnp.where(lane < row, lengths, 0), axis=1, keepdims=True)
    ends = starts + jnp.sum(jnp.where(lane == row, lengths, 0), axis=1, keepdims=True)
    column = iota((requests, positions), 1)
    inside = (column >= 2 * starts) & (column < 2 * ends) & (column % 2 == 0)
    bias = jnp.where(inside, 0.0, -jnp.inf).astype(F32)
    bias = jnp.concatenate([bias] * groups, axis=0)
    copies[1].wait()
    queries = queries_ref[...].astype(F32)
    copies[3].wait()
    for head in range(KV_HEADS):
        wide_ref[head] = own_ref[:, head * HEAD_DIM:(head + 1) * HEAD_DIM].astype(F32)
    copies[2].wait()
    heads = range(KV_HEADS)
    blocks = [kv_ref[:, head * HEAD_DIM:(head + 1) * HEAD_DIM] for head in heads]
    stacks = []
    for head in heads:
        at = head * groups * HEAD_DIM
        stacks.append(jnp.concatenate([queries[:, at + j * HEAD_DIM:at + (j + 1) * HEAD_DIM] for j in range(groups)], axis=0))
    keys = [jnp.concatenate([wide_ref[head, pl.ds(0, requests, stride=2), :]] * groups, axis=0) for head in heads]
    raw = [lax.dot_general(s.astype(BF16), k, NT, preferred_element_type=F32) for s, k in zip(stacks, blocks)]
    own_scores = [jnp.sum(s * k, axis=1, keepdims=True) * scale for s, k in zip(stacks, keys)]
    weights, own_weights = [], []
    for r, own_score in zip(raw, own_scores):
        scores = r * scale + bias
        peak = jnp.maximum(jnp.max(scores, axis=1, keepdims=True), own_score)
        expos = jnp.exp(scores - peak)
        own_expo = jnp.exp(own_score - peak)
        total = jnp.sum(expos, axis=1, keepdims=True) + own_expo
        weights.append(pltpu.roll(expos / total, 1, 1).astype(BF16))
        own_weights.append((own_expo / total).astype(BF16).astype(F32))
    sums = [jnp.dot(w, k, preferred_element_type=F32) for w, k in zip(weights, blocks)]
    for head, summed, own_weight in zip(heads, sums, own_weights):
        summed = summed + own_weight * jnp.concatenate([wide_ref[head, pl.ds(1, requests, stride=2), :]] * groups, axis=0)
        for j in range(groups):
            at = (head * groups + j) * HEAD_DIM
            att_ref[:, at:at + HEAD_DIM] = summed[j * requests:(j + 1) * requests].astype(BF16).astype(F32)
    copies[4].wait()
    residual = hidden_ref[...].astype(F32) + att_ref[...]
    residual_ref[...] = residual
    centered = residual - jnp.mean(residual, axis=1, keepdims=True)
    spread_of = jnp.mean(centered * centered, axis=1, keepdims=True)
    copies[5].wait()
    normed = (centered * lax.rsqrt(spread_of + EPSILON) * gain_ref[...]).astype(BF16)
    normed_ref[...] = normed
    copies[6].wait()
    mine = half()
    capacity = near_ref.shape[0]
    slot = iota((capacity, requests), 0).astype(F32)
    for expert, out in ((mine, near_ref), (1 - mine, far_ref)):
        named, before = slot_rows(routes_ref[...], expert)
        placing = jnp.where(before == slot, named, 0.0).astype(BF16)
        out[...] = jnp.dot(placing, normed, preferred_element_type=F32).astype(BF16)


def gate_mix(half, normed_ref, router_ref, routes_ref, capacity):
    routes = routes_ref[...]
    fanout, requests = routes.shape
    experts = router_ref.shape[0]
    logits = lax.dot_general(normed_ref[...], router_ref[...], NT, preferred_element_type=F32)
    lane = iota((requests, experts), 1).astype(F32)
    columns = [to_column(routes[k:k + 1].astype(F32)) for k in range(fanout)]
    routed = [jnp.sum(jnp.where(lane == columns[k], logits, 0.0), axis=1, keepdims=True) for k in range(fanout)]
    gates = [1.0 / sum(jnp.exp(routed[j] - routed[k]) for j in range(fanout)) for k in range(fanout)]
    mine = half()
    column = iota((requests, FLIGHT * capacity), 1)
    mix = jnp.zeros((requests, FLIGHT * capacity), F32)
    for turn, expert in enumerate((mine, 1 - mine)):
        named, before = slot_rows(routes, expert)
        named, before = to_column(named), to_column(before)
        gate = jnp.zeros((requests, 1), F32)
        for k in range(fanout):
            gate = jnp.where(columns[k] == expert.astype(F32), gates[k], gate)
        place = (column - turn * capacity).astype(F32)
        mix = jnp.where((before == place) & (named > 0.0), gate, mix)
    return mix


def join_kernel(near_ref, arrived_ref, out_ref):
    out_ref[...] = jnp.concatenate([near_ref[...], arrived_ref[...]], axis=0)


def project(inner_ref, down_ref, keep_ref, send_ref, start):
    rows = inner_ref[...]
    half = rows.shape[0] // 2
    doubled = jnp.concatenate([rows, rows], axis=0)
    width = keep_ref.shape[1]
    part = 1024 if width % 1024 == 0 else width
    for i in range(width // part):
        at = slice(i * part, (i + 1) * part)
        out = jnp.dot(doubled, down_ref[:, start + i * part:start + (i + 1) * part], preferred_element_type=F32)
        keep_ref[:, at] = out[:half]
        send_ref[:, at] = out[half:2 * half].astype(BF16)


def expert_kernel(chips, chunk, *refs):
    pieces = refs[:2 * chips]
    gate_ref, up_ref, down_ref, inner_ref, keep_ref, send_ref, rows_ref = refs[2 * chips:]
    hidden, width = gate_ref.shape
    count = pieces[0].shape[0]
    for i, piece in enumerate(pieces):
        rows_ref[i * count:(i + 1) * count, :] = piece[...]
    for i in range(hidden // chunk):
        at = slice(i * chunk, (i + 1) * chunk)
        rows = rows_ref[...]
        gate_part = lax.dot_general(gate_ref[at], rows, NT, preferred_element_type=F32)
        up_part = lax.dot_general(up_ref[at], rows, NT, preferred_element_type=F32)
        inner = gate_part / (1.0 + jnp.exp(-gate_part)) * up_part
        inner_ref[:, at] = inner.T.astype(BF16)
    project(inner_ref, down_ref, keep_ref, send_ref, 0)


def rest_kernel(start, inner_ref, down_ref, keep_ref, send_ref):
    project(inner_ref, down_ref, keep_ref, send_ref, start)


def core_sum_kernel(keep_ref, recv_ref, keep_rest_ref, recv_rest_ref, near_ref, far_ref, *rest):
    capacity = near_ref.shape[0]
    start = keep_ref.shape[1]
    for keep, recv, at in (
        (keep_ref, recv_ref, slice(0, start)),
        (keep_rest_ref, recv_rest_ref, slice(start, near_ref.shape[1])),
    ):
        total = keep[...] + recv[...].astype(F32)
        for i, out in enumerate((near_ref, far_ref) + rest):
            out[:, at] = total[i * capacity:(i + 1) * capacity].astype(out.dtype)


def far_sum_kernel(far_ref, *refs):
    *parts, out_ref = refs
    total = far_ref[...]
    for part in parts:
        total = total + part[...].astype(F32)
    out_ref[...] = total.astype(BF16)


def weighted(mix, rows, start):
    terms = [mix[:, start + j:start + j + 1] * rows[j:j + 1] for j in range(rows.shape[0])]
    return sum(terms[1:], terms[0])


def near_kernel(half, residual_ref, normed_ref, router_ref, routes_ref, near_ref, *refs):
    *parts, base_ref, mix_ref = refs
    mix = gate_mix(half, normed_ref, router_ref, routes_ref, near_ref.shape[0])
    mix_ref[...] = mix
    total = near_ref[...]
    for part in parts:
        total = total + part[...].astype(F32)
    base_ref[...] = residual_ref[...] + weighted(mix, total.astype(BF16).astype(F32), 0)


def mix_kernel(base_ref, mix_ref, far_ref, out_ref):
    rows = far_ref[...].astype(F32)
    out_ref[...] = (base_ref[...] + weighted(mix_ref[...], rows, rows.shape[0])).astype(BF16)


def like(*shape, dtype=BF16):
    return jax.ShapeDtypeStruct(shape, dtype)


def params(mib):
    return pltpu.CompilerParams(vmem_limit_bytes=mib * MIB)


def body(
    hidden_state,
    queries,
    new_entries,
    cached,
    cache_lengths,
    routes,
    norm_gain,
    router_weight,
    expert_gate,
    expert_up,
    expert_down,
):
    requests, width = hidden_state.shape
    devices = lax.axis_size("pool")
    group = devices // FLIGHT
    chips = group // CORES
    experts = router_weight.shape[1]
    fanout = routes.shape[1]
    capacity = min(requests, 2 * requests * fanout // experts)
    count = 2 * capacity
    hidden = expert_gate.shape[2]

    tight = 6 * hidden * width > 24 * MIB

    def half():
        return lax.axis_index("pool") // group

    def exchange(value, bit):
        return lax.ppermute(value, "pool", [(i, i ^ bit) for i in range(devices)])

    positions = cached.shape[0]
    heads = cached.shape[2]
    weights = [
        pltpu.with_memory_space_constraint(w, pltpu.VMEM)
        for w in (jnp.swapaxes(expert_gate, 1, 2)[0], jnp.swapaxes(expert_up, 1, 2)[0], expert_down[0])
    ]
    routes = routes.T
    front = (hidden_state, queries, cached, new_entries, cache_lengths, routes, norm_gain[None])
    residual, normed, near, far = pl.pallas_call(
        functools.partial(front_kernel, half),
        out_shape=(like(requests, width, dtype=F32), like(requests, width), like(capacity, width), like(capacity, width)),
        in_specs=[whole(pltpu.HBM)] * 7,
        out_specs=(whole(),) * 4,
        scratch_shapes=[
            pltpu.VMEM((requests, width), BF16),
            pltpu.VMEM((requests, width), BF16),
            pltpu.VMEM((2 * positions, heads), BF16),
            pltpu.VMEM((2 * requests, heads), BF16),
            pltpu.VMEM((1, requests), jnp.int32),
            pltpu.VMEM((fanout, requests), jnp.int32),
            pltpu.VMEM((1, width), F32),
            pltpu.VMEM((KV_HEADS, 2 * requests, HEAD_DIM), F32),
            pltpu.VMEM((requests, width), F32),
            pltpu.SemaphoreType.DMA((7,)),
        ],
        compiler_params=params(2 if tight else 24),
        cost_estimate=pl.CostEstimate(flops=200_000_000_000, bytes_accessed=50_000_000, transcendentals=0),
    )(*(pltpu.with_memory_space_constraint(x, pltpu.HBM) for x in front))
    arrived = exchange(far, group)
    own = pl.pallas_call(
        join_kernel,
        out_shape=like(count, width),
        in_specs=[whole()] * 2,
        out_specs=whole(),
        compiler_params=params(2 if tight else 24),
    )(near, arrived)
    mine = [own] + [exchange(own, CORES * j) for j in range(1, chips)]
    beside = [exchange(piece, 1) for piece in mine]
    chunk = hidden // 6 if hidden % 96 == 0 else hidden
    steps = hidden // chunk
    rows = chips * count
    start = 2 * width // 3 // 1024 * 1024
    inner, keep, send = pl.pallas_call(
        functools.partial(expert_kernel, chips, chunk),
        out_shape=(like(2 * rows, hidden), like(rows, start, dtype=F32), like(rows, start)),
        in_specs=[whole()] * (2 * chips + 3),
        out_specs=(whole(),) * 3,
        scratch_shapes=[pltpu.VMEM((2 * rows, width), BF16)],
        compiler_params=params(3 if tight else 24),
    )(*mine, *beside, *weights)
    recv = exchange(send, 1)
    keep_rest, send_rest = pl.pallas_call(
        functools.partial(rest_kernel, start),
        out_shape=(like(rows, width - start, dtype=F32), like(rows, width - start)),
        in_specs=[whole()] * 2,
        out_specs=(whole(),) * 2,
        compiler_params=params(2 if tight else 24),
    )(inner, weights[2])
    recv_rest = exchange(send_rest, 1)
    in_vmem = [pltpu.with_memory_space_constraint(x, pltpu.VMEM) for x in (keep, recv, keep_rest, recv_rest)]
    near_sum, far_sum, *rest = pl.pallas_call(
        core_sum_kernel,
        out_shape=(like(capacity, width, dtype=F32),) * 2 + (like(capacity, width),) * (2 * chips - 2),
        in_specs=[whole()] * 4,
        out_specs=(whole(),) * (2 * chips),
        compiler_params=params(2 if tight else 24),
    )(*in_vmem)
    order = range(chips - 1, 0, -1)
    far_parts = [exchange(rest[2 * j - 1], CORES * j) for j in order]
    near_parts = [exchange(rest[2 * j - 2], CORES * j) for j in order]
    far_out = pl.pallas_call(
        far_sum_kernel,
        out_shape=like(capacity, width),
        in_specs=[whole()] * chips,
        out_specs=whole(),
        compiler_params=params(2 if tight else 24),
    )(far_sum, *far_parts)
    back = exchange(far_out, group)
    base, mix = pl.pallas_call(
        functools.partial(near_kernel, half),
        out_shape=(like(requests, width, dtype=F32), like(requests, count, dtype=F32)),
        in_specs=[whole()] * (4 + chips),
        out_specs=(whole(),) * 2,
        compiler_params=params(2 if tight else 24),
    )(residual, normed, router_weight.T, routes, near_sum, *near_parts)
    return pl.pallas_call(
        mix_kernel,
        out_shape=like(requests, width),
        in_specs=[whole()] * 3,
        out_specs=whole(),
        compiler_params=params(2 if tight else 24),
    )(base, mix, back)


def solution(mesh):
    in_specs = (
        P(("rep", "pool"), None),
        P(("rep", "pool"), None),
        P(("rep", "pool"), None, None),
        P(("rep", "pool"), None, None),
        P(("rep", "pool"), None),
        P(("rep", "pool"), None),
        P(),
        P(),
        P("pool", None, None),
        P("pool", None, None),
        P("pool", None, None),
    )
    out_specs = P(("rep", "pool"), None)
    return jax.shard_map(body, mesh=mesh, in_specs=in_specs, out_specs=out_specs, check_vma=False)
```

```python
import functools
import math

import jax
import jax.numpy as jnp
from jax import lax
from jax.experimental import pallas as pl
from jax.experimental.pallas import tpu as pltpu
from jax.sharding import PartitionSpec as P

HEADS = 48
KV_HEADS = 8
HEAD_DIM = 128
FLIGHT = 2
CORES = 2
EPSILON = 1e-05

F32 = jnp.float32
BF16 = jnp.bfloat16
NT = (((1,), (1,)), ((), ()))
TN = (((0,), (0,)), ((), ()))
MIB = 1 << 20


def whole(space=pltpu.VMEM):
    return pl.BlockSpec(memory_space=space)


def iota(shape, dim):
    return lax.broadcasted_iota(jnp.int32, shape, dim)


def spread(rows):
    n = rows.shape[1]
    return jnp.broadcast_to(rows, (n, n)), iota((n, n), 0), iota((n, n), 1)


def to_column(values):
    wide, row, lane = spread(values)
    return jnp.sum(jnp.where(row == lane, wide, 0.0), axis=1, keepdims=True)


def slot_rows(routes, expert):
    named = jnp.max((routes == expert).astype(F32), axis=0, keepdims=True)
    column = to_column(named)
    _, row, lane = spread(named)
    before = jnp.sum(jnp.where(row < lane, column, 0.0), axis=0, keepdims=True)
    return named, before


def front_kernel(half, hidden_hbm, queries_hbm, cached_hbm, own_hbm, lengths_hbm, routes_hbm, gain_hbm,
                 residual_ref, normed_ref, near_ref, far_ref,
                 hidden_ref, queries_ref, kv_ref, own_ref, lengths_ref, routes_ref, gain_ref, wide_ref, att_ref, sems):
    pairs = (
        (lengths_hbm, lengths_ref),
        (queries_hbm, queries_ref),
        (cached_hbm.reshape(kv_ref.shape), kv_ref),
        (own_hbm.reshape(own_ref.shape), own_ref),
        (hidden_hbm, hidden_ref),
        (gain_hbm, gain_ref),
        (routes_hbm, routes_ref),
    )
    copies = [pltpu.make_async_copy(src, dst, sems.at[i]) for i, (src, dst) in enumerate(pairs)]
    for copy in copies:
        copy.start()
    requests, width = hidden_ref.shape
    groups = HEADS // KV_HEADS
    positions = kv_ref.shape[0]
    scale = 1.0 / math.sqrt(HEAD_DIM)
    row, lane = iota((requests, requests), 0), iota((requests, requests), 1)
    copies[0].wait()
    lengths = jnp.broadcast_to(lengths_ref[...], (requests, requests))
    starts = jnp.sum(jnp.where(lane < row, lengths, 0), axis=1, keepdims=True)
    ends = starts + jnp.sum(jnp.where(lane == row, lengths, 0), axis=1, keepdims=True)
    column = iota((requests, positions), 1)
    inside = (column >= 2 * starts) & (column < 2 * ends) & (column % 2 == 0)
    bias = jnp.where(inside, 0.0, -jnp.inf).astype(F32)
    bias = jnp.concatenate([bias] * groups, axis=0)
    copies[1].wait()
    queries = queries_ref[...].astype(F32)
    copies[3].wait()
    for head in range(KV_HEADS):
        wide_ref[head] = own_ref[:, head * HEAD_DIM:(head + 1) * HEAD_DIM].astype(F32)
    copies[2].wait()
    heads = range(KV_HEADS)
    blocks = [kv_ref[:, head * HEAD_DIM:(head + 1) * HEAD_DIM] for head in heads]
    stacks = []
    for head in heads:
        at = head * groups * HEAD_DIM
        stacks.append(jnp.concatenate([queries[:, at + j * HEAD_DIM:at + (j + 1) * HEAD_DIM] for j in range(groups)], axis=0))
    keys = [jnp.concatenate([wide_ref[head, pl.ds(0, requests, stride=2), :]] * groups, axis=0) for head in heads]
    raw = [lax.dot_general(s.astype(BF16), k, NT, preferred_element_type=F32) for s, k in zip(stacks, blocks)]
    own_scores = [jnp.sum(s * k, axis=1, keepdims=True) * scale for s, k in zip(stacks, keys)]
    weights, own_weights = [], []
    for r, own_score in zip(raw, own_scores):
        scores = r * scale + bias
        peak = jnp.maximum(jnp.max(scores, axis=1, keepdims=True), own_score)
        expos = jnp.exp(scores - peak)
        own_expo = jnp.exp(own_score - peak)
        total = jnp.sum(expos, axis=1, keepdims=True) + own_expo
        weights.append(pltpu.roll(expos / total, 1, 1).astype(BF16))
        own_weights.append((own_expo / total).astype(BF16).astype(F32))
    sums = [jnp.dot(w, k, preferred_element_type=F32) for w, k in zip(weights, blocks)]
    for head, summed, own_weight in zip(heads, sums, own_weights):
        summed = summed + own_weight * jnp.concatenate([wide_ref[head, pl.ds(1, requests, stride=2), :]] * groups, axis=0)
        for j in range(groups):
            at = (head * groups + j) * HEAD_DIM
            att_ref[:, at:at + HEAD_DIM] = summed[j * requests:(j + 1) * requests].astype(BF16).astype(F32)
    copies[4].wait()
    residual = hidden_ref[...].astype(F32) + att_ref[...]
    residual_ref[...] = residual
    centered = residual - jnp.mean(residual, axis=1, keepdims=True)
    spread_of = jnp.mean(centered * centered, axis=1, keepdims=True)
    copies[5].wait()
    normed = (centered * lax.rsqrt(spread_of + EPSILON) * gain_ref[...]).astype(BF16)
    normed_ref[...] = normed
    copies[6].wait()
    mine = half()
    capacity = near_ref.shape[0]
    slot = iota((capacity, requests), 0).astype(F32)
    for expert, out in ((mine, near_ref), (1 - mine, far_ref)):
        named, before = slot_rows(routes_ref[...], expert)
        placing = jnp.where(before == slot, named, 0.0).astype(BF16)
        out[...] = jnp.dot(placing, normed, preferred_element_type=F32).astype(BF16)


def gate_mix(half, normed_ref, router_ref, routes_ref, capacity):
    routes = routes_ref[...]
    fanout, requests = routes.shape
    experts = router_ref.shape[0]
    logits = lax.dot_general(normed_ref[...], router_ref[...], NT, preferred_element_type=F32)
    lane = iota((requests, experts), 1).astype(F32)
    columns = [to_column(routes[k:k + 1].astype(F32)) for k in range(fanout)]
    routed = [jnp.sum(jnp.where(lane == columns[k], logits, 0.0), axis=1, keepdims=True) for k in range(fanout)]
    gates = [1.0 / sum(jnp.exp(routed[j] - routed[k]) for j in range(fanout)) for k in range(fanout)]
    mine = half()
    column = iota((requests, FLIGHT * capacity), 1)
    mix = jnp.zeros((requests, FLIGHT * capacity), F32)
    for turn, expert in enumerate((mine, 1 - mine)):
        named, before = slot_rows(routes, expert)
        named, before = to_column(named), to_column(before)
        gate = jnp.zeros((requests, 1), F32)
        for k in range(fanout):
            gate = jnp.where(columns[k] == expert.astype(F32), gates[k], gate)
        place = (column - turn * capacity).astype(F32)
        mix = jnp.where((before == place) & (named > 0.0), gate, mix)
    return mix


def join_kernel(near_ref, arrived_ref, out_ref):
    out_ref[...] = jnp.concatenate([near_ref[...], arrived_ref[...]], axis=0)


def project(inner_ref, down_ref, keep_ref, send_ref, start):
    rows = inner_ref[...]
    half = rows.shape[0] // 2
    doubled = jnp.concatenate([rows, rows], axis=0)
    width = keep_ref.shape[1]
    part = 1024 if width % 1024 == 0 else width
    for i in range(width // part):
        at = slice(i * part, (i + 1) * part)
        out = jnp.dot(doubled, down_ref[:, start + i * part:start + (i + 1) * part], preferred_element_type=F32)
        keep_ref[:, at] = out[:half]
        send_ref[:, at] = out[half:2 * half].astype(BF16)


def expert_kernel(chips, chunk, depth, *refs):
    pieces = refs[:2 * chips]
    gate_ref, up_ref, down_ref, inner_ref, keep_ref, send_ref, rows_ref = refs[2 * chips:]
    hidden, width = gate_ref.shape
    count = pieces[0].shape[0]
    for i, piece in enumerate(pieces):
        rows_ref[i * count:(i + 1) * count, :] = piece[...]
    for i in range(hidden // chunk):
        at = slice(i * chunk, (i + 1) * chunk)
        gate_part = jnp.zeros((rows_ref.shape[0], chunk), F32)
        up_part = jnp.zeros((chunk, rows_ref.shape[0]), F32)
        for k in range(0, width, depth):
            rows = rows_ref[:, k:k + depth]
            gate_part += lax.dot_general(rows, gate_ref[at, k:k + depth], NT, preferred_element_type=F32)
            up_part += lax.dot_general(up_ref[at, k:k + depth], rows, NT, preferred_element_type=F32)
        inner_ref[:, at] = (gate_part / (1.0 + jnp.exp(-gate_part)) * up_part.T).astype(BF16)
    project(inner_ref, down_ref, keep_ref, send_ref, 0)


def rest_kernel(start, inner_ref, down_ref, keep_ref, send_ref):
    project(inner_ref, down_ref, keep_ref, send_ref, start)


def core_sum_kernel(keep_ref, recv_ref, keep_rest_ref, recv_rest_ref, near_ref, far_ref, *rest):
    capacity = near_ref.shape[0]
    start = keep_ref.shape[1]
    for keep, recv, at in (
        (keep_ref, recv_ref, slice(0, start)),
        (keep_rest_ref, recv_rest_ref, slice(start, near_ref.shape[1])),
    ):
        total = keep[...] + recv[...].astype(F32)
        for i, out in enumerate((near_ref, far_ref) + rest):
            out[:, at] = total[i * capacity:(i + 1) * capacity].astype(out.dtype)


def far_sum_kernel(far_ref, *refs):
    *parts, out_ref = refs
    total = far_ref[...]
    for part in parts:
        total = total + part[...].astype(F32)
    out_ref[...] = total.astype(BF16)


def weighted(mix, rows, start):
    terms = [mix[:, start + j:start + j + 1] * rows[j:j + 1] for j in range(rows.shape[0])]
    return sum(terms[1:], terms[0])


def near_kernel(half, residual_ref, normed_ref, router_ref, routes_ref, near_ref, *refs):
    *parts, base_ref, mix_ref = refs
    mix = gate_mix(half, normed_ref, router_ref, routes_ref, near_ref.shape[0])
    mix_ref[...] = mix
    total = near_ref[...]
    for part in parts:
        total = total + part[...].astype(F32)
    base_ref[...] = residual_ref[...] + weighted(mix, total.astype(BF16).astype(F32), 0)


def mix_kernel(base_ref, mix_ref, far_ref, out_ref):
    rows = far_ref[...].astype(F32)
    out_ref[...] = (base_ref[...] + weighted(mix_ref[...], rows, rows.shape[0])).astype(BF16)


def like(*shape, dtype=BF16):
    return jax.ShapeDtypeStruct(shape, dtype)


def params(mib):
    return pltpu.CompilerParams(vmem_limit_bytes=mib * MIB)


def body(
    hidden_state,
    queries,
    new_entries,
    cached,
    cache_lengths,
    routes,
    norm_gain,
    router_weight,
    expert_gate,
    expert_up,
    expert_down,
):
    requests, width = hidden_state.shape
    devices = lax.axis_size("pool")
    group = devices // FLIGHT
    chips = group // CORES
    experts = router_weight.shape[1]
    fanout = routes.shape[1]
    capacity = min(requests, 2 * requests * fanout // experts)
    count = 2 * capacity
    hidden = expert_gate.shape[2]

    tight = 6 * hidden * width > 24 * MIB

    def half():
        return lax.axis_index("pool") // group

    def exchange(value, bit):
        return lax.ppermute(value, "pool", [(i, i ^ bit) for i in range(devices)])

    positions = cached.shape[0]
    heads = cached.shape[2]
    weights = [
        pltpu.with_memory_space_constraint(w, pltpu.VMEM)
        for w in (jnp.swapaxes(expert_gate, 1, 2)[0], jnp.swapaxes(expert_up, 1, 2)[0], expert_down[0])
    ]
    routes = routes.T
    front = (hidden_state, queries, cached, new_entries, cache_lengths, routes, norm_gain[None])
    residual, normed, near, far = pl.pallas_call(
        functools.partial(front_kernel, half),
        out_shape=(like(requests, width, dtype=F32), like(requests, width), like(capacity, width), like(capacity, width)),
        in_specs=[whole(pltpu.HBM)] * 7,
        out_specs=(whole(),) * 4,
        scratch_shapes=[
            pltpu.VMEM((requests, width), BF16),
            pltpu.VMEM((requests, width), BF16),
            pltpu.VMEM((2 * positions, heads), BF16),
            pltpu.VMEM((2 * requests, heads), BF16),
            pltpu.VMEM((1, requests), jnp.int32),
            pltpu.VMEM((fanout, requests), jnp.int32),
            pltpu.VMEM((1, width), F32),
            pltpu.VMEM((KV_HEADS, 2 * requests, HEAD_DIM), F32),
            pltpu.VMEM((requests, width), F32),
            pltpu.SemaphoreType.DMA((7,)),
        ],
        compiler_params=params(2 if tight else 24),
        cost_estimate=pl.CostEstimate(flops=200_000_000_000, bytes_accessed=50_000_000, transcendentals=0),
    )(*(pltpu.with_memory_space_constraint(x, pltpu.HBM) for x in front))
    arrived = exchange(far, group)
    own = pl.pallas_call(
        join_kernel,
        out_shape=like(count, width),
        in_specs=[whole()] * 2,
        out_specs=whole(),
        compiler_params=params(2 if tight else 24),
    )(near, arrived)
    mine = [own] + [exchange(own, CORES * j) for j in range(1, chips)]
    beside = [exchange(piece, 1) for piece in mine]
    chunk = 336 if hidden % 336 == 0 else hidden
    depth = 256 if width % 256 == 0 else width
    rows = chips * count
    start = 2 * width // 3 // 1024 * 1024
    inner, keep, send = pl.pallas_call(
        functools.partial(expert_kernel, chips, chunk, depth),
        out_shape=(like(2 * rows, hidden), like(rows, start, dtype=F32), like(rows, start)),
        in_specs=[whole()] * (2 * chips + 3),
        out_specs=(whole(),) * 3,
        scratch_shapes=[pltpu.VMEM((2 * rows, width), BF16)],
        compiler_params=params(3 if tight else 24),
    )(*mine, *beside, *weights)
    recv = exchange(send, 1)
    keep_rest, send_rest = pl.pallas_call(
        functools.partial(rest_kernel, start),
        out_shape=(like(rows, width - start, dtype=F32), like(rows, width - start)),
        in_specs=[whole()] * 2,
        out_specs=(whole(),) * 2,
        compiler_params=params(2 if tight else 24),
    )(inner, weights[2])
    recv_rest = exchange(send_rest, 1)
    in_vmem = [pltpu.with_memory_space_constraint(x, pltpu.VMEM) for x in (keep, recv, keep_rest, recv_rest)]
    near_sum, far_sum, *rest = pl.pallas_call(
        core_sum_kernel,
        out_shape=(like(capacity, width, dtype=F32),) * 2 + (like(capacity, width),) * (2 * chips - 2),
        in_specs=[whole()] * 4,
        out_specs=(whole(),) * (2 * chips),
        compiler_params=params(2 if tight else 24),
    )(*in_vmem)
    order = range(chips - 1, 0, -1)
    far_parts = [exchange(rest[2 * j - 1], CORES * j) for j in order]
    near_parts = [exchange(rest[2 * j - 2], CORES * j) for j in order]
    far_out = pl.pallas_call(
        far_sum_kernel,
        out_shape=like(capacity, width),
        in_specs=[whole()] * chips,
        out_specs=whole(),
        compiler_params=params(2 if tight else 24),
    )(far_sum, *far_parts)
    back = exchange(far_out, group)
    base, mix = pl.pallas_call(
        functools.partial(near_kernel, half),
        out_shape=(like(requests, width, dtype=F32), like(requests, count, dtype=F32)),
        in_specs=[whole()] * (4 + chips),
        out_specs=(whole(),) * 2,
        compiler_params=params(2 if tight else 24),
    )(residual, normed, router_weight.T, routes, near_sum, *near_parts)
    return pl.pallas_call(
        mix_kernel,
        out_shape=like(requests, width),
        in_specs=[whole()] * 3,
        out_specs=whole(),
        compiler_params=params(2 if tight else 24),
    )(base, mix, back)


def solution(mesh):
    in_specs = (
        P(("rep", "pool"), None),
        P(("rep", "pool"), None),
        P(("rep", "pool"), None, None),
        P(("rep", "pool"), None, None),
        P(("rep", "pool"), None),
        P(("rep", "pool"), None),
        P(),
        P(),
        P("pool", None, None),
        P("pool", None, None),
        P("pool", None, None),
    )
    out_specs = P(("rep", "pool"), None)
    return jax.shard_map(body, mesh=mesh, in_specs=in_specs, out_specs=out_specs, check_vma=False)
```

```python
import functools
import math

import jax
import jax.numpy as jnp
from jax import lax
from jax.experimental import pallas as pl
from jax.experimental.pallas import tpu as pltpu
from jax.sharding import PartitionSpec as P

HEADS = 48
KV_HEADS = 8
HEAD_DIM = 128
FLIGHT = 2
CORES = 2
EPSILON = 1e-05

F32 = jnp.float32
BF16 = jnp.bfloat16
NT = (((1,), (1,)), ((), ()))
TN = (((0,), (0,)), ((), ()))
MIB = 1 << 20


def whole(space=pltpu.VMEM):
    return pl.BlockSpec(memory_space=space)


def iota(shape, dim):
    return lax.broadcasted_iota(jnp.int32, shape, dim)


def spread(rows):
    n = rows.shape[1]
    return jnp.broadcast_to(rows, (n, n)), iota((n, n), 0), iota((n, n), 1)


def to_column(values):
    wide, row, lane = spread(values)
    return jnp.sum(jnp.where(row == lane, wide, 0.0), axis=1, keepdims=True)


def slot_rows(routes, expert):
    named = jnp.max((routes == expert).astype(F32), axis=0, keepdims=True)
    column = to_column(named)
    _, row, lane = spread(named)
    before = jnp.sum(jnp.where(row < lane, column, 0.0), axis=0, keepdims=True)
    return named, before


def front_kernel(half, hidden_hbm, queries_hbm, cached_hbm, own_hbm, lengths_hbm, routes_hbm, gain_hbm,
                 residual_ref, normed_ref, near_ref, far_ref,
                 hidden_ref, queries_ref, kv_ref, own_ref, lengths_ref, routes_ref, gain_ref, wide_ref, att_ref, sems):
    pairs = (
        (lengths_hbm, lengths_ref),
        (queries_hbm, queries_ref),
        (cached_hbm.reshape(kv_ref.shape), kv_ref),
        (own_hbm.reshape(own_ref.shape), own_ref),
        (hidden_hbm, hidden_ref),
        (gain_hbm, gain_ref),
        (routes_hbm, routes_ref),
    )
    copies = [pltpu.make_async_copy(src, dst, sems.at[i]) for i, (src, dst) in enumerate(pairs)]
    for copy in copies:
        copy.start()
    requests, width = hidden_ref.shape
    groups = HEADS // KV_HEADS
    positions = kv_ref.shape[0]
    scale = 1.0 / math.sqrt(HEAD_DIM)
    row, lane = iota((requests, requests), 0), iota((requests, requests), 1)
    copies[0].wait()
    lengths = jnp.broadcast_to(lengths_ref[...], (requests, requests))
    starts = jnp.sum(jnp.where(lane < row, lengths, 0), axis=1, keepdims=True)
    ends = starts + jnp.sum(jnp.where(lane == row, lengths, 0), axis=1, keepdims=True)
    column = iota((requests, positions), 1)
    inside = (column >= 2 * starts) & (column < 2 * ends) & (column % 2 == 0)
    bias = jnp.where(inside, 0.0, -jnp.inf).astype(F32)
    bias = jnp.concatenate([bias] * groups, axis=0)
    copies[1].wait()
    queries = queries_ref[...].astype(F32)
    copies[3].wait()
    for head in range(KV_HEADS):
        wide_ref[head] = own_ref[:, head * HEAD_DIM:(head + 1) * HEAD_DIM].astype(F32)
    copies[2].wait()
    heads = range(KV_HEADS)
    blocks = [kv_ref[:, head * HEAD_DIM:(head + 1) * HEAD_DIM] for head in heads]
    stacks = []
    for head in heads:
        at = head * groups * HEAD_DIM
        stacks.append(jnp.concatenate([queries[:, at + j * HEAD_DIM:at + (j + 1) * HEAD_DIM] for j in range(groups)], axis=0))
    keys = [jnp.concatenate([wide_ref[head, pl.ds(0, requests, stride=2), :]] * groups, axis=0) for head in heads]
    raw = [lax.dot_general(s.astype(BF16), k, NT, preferred_element_type=F32) for s, k in zip(stacks, blocks)]
    own_scores = [jnp.sum(s * k, axis=1, keepdims=True) * scale for s, k in zip(stacks, keys)]
    weights, own_weights = [], []
    for r, own_score in zip(raw, own_scores):
        scores = r * scale + bias
        peak = jnp.maximum(jnp.max(scores, axis=1, keepdims=True), own_score)
        expos = jnp.exp(scores - peak)
        own_expo = jnp.exp(own_score - peak)
        total = jnp.sum(expos, axis=1, keepdims=True) + own_expo
        weights.append(pltpu.roll(expos / total, 1, 1).astype(BF16))
        own_weights.append((own_expo / total).astype(BF16).astype(F32))
    sums = [jnp.dot(w, k, preferred_element_type=F32) for w, k in zip(weights, blocks)]
    for head, summed, own_weight in zip(heads, sums, own_weights):
        summed = summed + own_weight * jnp.concatenate([wide_ref[head, pl.ds(1, requests, stride=2), :]] * groups, axis=0)
        for j in range(groups):
            at = (head * groups + j) * HEAD_DIM
            att_ref[:, at:at + HEAD_DIM] = summed[j * requests:(j + 1) * requests].astype(BF16).astype(F32)
    copies[4].wait()
    residual = hidden_ref[...].astype(F32) + att_ref[...]
    residual_ref[...] = residual
    centered = residual - jnp.mean(residual, axis=1, keepdims=True)
    spread_of = jnp.mean(centered * centered, axis=1, keepdims=True)
    copies[5].wait()
    normed = (centered * lax.rsqrt(spread_of + EPSILON) * gain_ref[...]).astype(BF16)
    normed_ref[...] = normed
    copies[6].wait()
    mine = half()
    capacity = near_ref.shape[0]
    slot = iota((capacity, requests), 0).astype(F32)
    for expert, out in ((mine, near_ref), (1 - mine, far_ref)):
        named, before = slot_rows(routes_ref[...], expert)
        placing = jnp.where(before == slot, named, 0.0).astype(BF16)
        out[...] = jnp.dot(placing, normed, preferred_element_type=F32).astype(BF16)


def gate_mix(half, normed_ref, router_ref, routes_ref, capacity):
    routes = routes_ref[...]
    fanout, requests = routes.shape
    experts = router_ref.shape[0]
    logits = lax.dot_general(normed_ref[...], router_ref[...], NT, preferred_element_type=F32)
    lane = iota((requests, experts), 1).astype(F32)
    columns = [to_column(routes[k:k + 1].astype(F32)) for k in range(fanout)]
    routed = [jnp.sum(jnp.where(lane == columns[k], logits, 0.0), axis=1, keepdims=True) for k in range(fanout)]
    gates = [1.0 / sum(jnp.exp(routed[j] - routed[k]) for j in range(fanout)) for k in range(fanout)]
    mine = half()
    column = iota((requests, FLIGHT * capacity), 1)
    mix = jnp.zeros((requests, FLIGHT * capacity), F32)
    for turn, expert in enumerate((mine, 1 - mine)):
        named, before = slot_rows(routes, expert)
        named, before = to_column(named), to_column(before)
        gate = jnp.zeros((requests, 1), F32)
        for k in range(fanout):
            gate = jnp.where(columns[k] == expert.astype(F32), gates[k], gate)
        place = (column - turn * capacity).astype(F32)
        mix = jnp.where((before == place) & (named > 0.0), gate, mix)
    return mix


def join_kernel(near_ref, arrived_ref, out_ref):
    out_ref[...] = jnp.concatenate([near_ref[...], arrived_ref[...]], axis=0)


def project(inner_ref, down_ref, keep_ref, send_ref, start):
    rows = inner_ref[...]
    half = rows.shape[0] // 2
    doubled = jnp.concatenate([rows, rows], axis=0)
    width = keep_ref.shape[1]
    part = 1024 if width % 1024 == 0 else width
    for i in range(width // part):
        at = slice(i * part, (i + 1) * part)
        out = jnp.dot(doubled, down_ref[:, start + i * part:start + (i + 1) * part], preferred_element_type=F32)
        keep_ref[:, at] = out[:half]
        send_ref[:, at] = out[half:2 * half].astype(BF16)


def expert_kernel(chips, chunk, depth, *refs):
    pieces = refs[:2 * chips]
    gate_ref, up_ref, inner_ref, rows_ref = refs[2 * chips:]
    hidden, width = gate_ref.shape
    count = pieces[0].shape[0]
    for i, piece in enumerate(pieces):
        rows_ref[i * count:(i + 1) * count, :] = piece[...]
    for i in range(hidden // chunk):
        at = slice(i * chunk, (i + 1) * chunk)
        gate_part = jnp.zeros((rows_ref.shape[0], chunk), F32)
        up_part = jnp.zeros((chunk, rows_ref.shape[0]), F32)
        for k in range(0, width, depth):
            rows = rows_ref[:, k:k + depth]
            gate_part += lax.dot_general(rows, gate_ref[at, k:k + depth], NT, preferred_element_type=F32)
            up_part += lax.dot_general(up_ref[at, k:k + depth], rows, NT, preferred_element_type=F32)
        inner_ref[:, at] = (gate_part / (1.0 + jnp.exp(-gate_part)) * up_part.T).astype(BF16)


def rest_kernel(start, inner_ref, down_ref, keep_ref, send_ref):
    project(inner_ref, down_ref, keep_ref, send_ref, start)


def core_sum_kernel(keep_ref, recv_ref, near_ref, far_ref, *rest):
    capacity = near_ref.shape[0]
    start = keep_ref.shape[1]
    for keep, recv, at in ((keep_ref, recv_ref, slice(0, start)),):
        total = keep[...] + recv[...].astype(F32)
        for i, out in enumerate((near_ref, far_ref) + rest):
            out[:, at] = total[i * capacity:(i + 1) * capacity].astype(out.dtype)


def far_sum_kernel(far_ref, *refs):
    *parts, out_ref = refs
    total = far_ref[...]
    for part in parts:
        total = total + part[...].astype(F32)
    out_ref[...] = total.astype(BF16)


def weighted(mix, rows, start):
    terms = [mix[:, start + j:start + j + 1] * rows[j:j + 1] for j in range(rows.shape[0])]
    return sum(terms[1:], terms[0])


def near_kernel(half, residual_ref, normed_ref, router_ref, routes_ref, near_ref, *refs):
    *parts, base_ref, mix_ref = refs
    mix = gate_mix(half, normed_ref, router_ref, routes_ref, near_ref.shape[0])
    mix_ref[...] = mix
    total = near_ref[...]
    for part in parts:
        total = total + part[...].astype(F32)
    base_ref[...] = residual_ref[...] + weighted(mix, total.astype(BF16).astype(F32), 0)


def mix_kernel(base_ref, mix_ref, far_ref, out_ref):
    rows = far_ref[...].astype(F32)
    out_ref[...] = (base_ref[...] + weighted(mix_ref[...], rows, rows.shape[0])).astype(BF16)


def like(*shape, dtype=BF16):
    return jax.ShapeDtypeStruct(shape, dtype)


def params(mib):
    return pltpu.CompilerParams(vmem_limit_bytes=mib * MIB)


def body(
    hidden_state,
    queries,
    new_entries,
    cached,
    cache_lengths,
    routes,
    norm_gain,
    router_weight,
    expert_gate,
    expert_up,
    expert_down,
):
    requests, width = hidden_state.shape
    devices = lax.axis_size("pool")
    group = devices // FLIGHT
    chips = group // CORES
    experts = router_weight.shape[1]
    fanout = routes.shape[1]
    capacity = min(requests, 2 * requests * fanout // experts)
    count = 2 * capacity
    hidden = expert_gate.shape[2]

    tight = 6 * hidden * width > 24 * MIB

    def half():
        return lax.axis_index("pool") // group

    def exchange(value, bit):
        return lax.ppermute(value, "pool", [(i, i ^ bit) for i in range(devices)])

    positions = cached.shape[0]
    heads = cached.shape[2]
    weights = [
        pltpu.with_memory_space_constraint(w, pltpu.VMEM)
        for w in (jnp.swapaxes(expert_gate, 1, 2)[0], jnp.swapaxes(expert_up, 1, 2)[0], expert_down[0])
    ]
    routes = routes.T
    front = (hidden_state, queries, cached, new_entries, cache_lengths, routes, norm_gain[None])
    residual, normed, near, far = pl.pallas_call(
        functools.partial(front_kernel, half),
        out_shape=(like(requests, width, dtype=F32), like(requests, width), like(capacity, width), like(capacity, width)),
        in_specs=[whole(pltpu.HBM)] * 7,
        out_specs=(whole(),) * 4,
        scratch_shapes=[
            pltpu.VMEM((requests, width), BF16),
            pltpu.VMEM((requests, width), BF16),
            pltpu.VMEM((2 * positions, heads), BF16),
            pltpu.VMEM((2 * requests, heads), BF16),
            pltpu.VMEM((1, requests), jnp.int32),
            pltpu.VMEM((fanout, requests), jnp.int32),
            pltpu.VMEM((1, width), F32),
            pltpu.VMEM((KV_HEADS, 2 * requests, HEAD_DIM), F32),
            pltpu.VMEM((requests, width), F32),
            pltpu.SemaphoreType.DMA((7,)),
        ],
        compiler_params=params(2 if tight else 24),
        cost_estimate=pl.CostEstimate(flops=200_000_000_000, bytes_accessed=50_000_000, transcendentals=0),
    )(*(pltpu.with_memory_space_constraint(x, pltpu.HBM) for x in front))
    arrived = exchange(far, group)
    own = pl.pallas_call(
        join_kernel,
        out_shape=like(count, width),
        in_specs=[whole()] * 2,
        out_specs=whole(),
        compiler_params=params(2 if tight else 24),
    )(near, arrived)
    mine = [own] + [exchange(own, CORES * j) for j in range(1, chips)]
    beside = [exchange(piece, 1) for piece in mine]
    chunk = 336 if hidden % 336 == 0 else hidden
    depth = 256 if width % 256 == 0 else width
    rows = chips * count
    start = 2 * width // 3 // 1024 * 1024
    inner = pl.pallas_call(
        functools.partial(expert_kernel, chips, chunk, depth),
        out_shape=like(2 * rows, hidden),
        in_specs=[whole()] * (2 * chips + 2),
        out_specs=whole(),
        scratch_shapes=[pltpu.VMEM((2 * rows, width), BF16)],
        compiler_params=params(2 if tight else 24),
    )(*mine, *beside, *weights[:2])

    def down(start, columns):
        return pl.pallas_call(
            functools.partial(rest_kernel, start),
            out_shape=(like(rows, columns, dtype=F32), like(rows, columns)),
            in_specs=[whole()] * 2,
            out_specs=(whole(),) * 2,
            compiler_params=params(2 if tight else 24),
        )(inner, weights[2])

    keep, send = down(0, width)
    recv = exchange(send, 1)
    in_vmem = [pltpu.with_memory_space_constraint(x, pltpu.VMEM) for x in (keep, recv)]
    near_sum, far_sum, *rest = pl.pallas_call(
        core_sum_kernel,
        out_shape=(like(capacity, width, dtype=F32),) * 2 + (like(capacity, width),) * (2 * chips - 2),
        in_specs=[whole()] * 2,
        out_specs=(whole(),) * (2 * chips),
        compiler_params=params(2 if tight else 24),
    )(*in_vmem)
    order = range(chips - 1, 0, -1)
    far_parts = [exchange(rest[2 * j - 1], CORES * j) for j in order]
    near_parts = [exchange(rest[2 * j - 2], CORES * j) for j in order]
    far_out = pl.pallas_call(
        far_sum_kernel,
        out_shape=like(capacity, width),
        in_specs=[whole()] * chips,
        out_specs=whole(),
        compiler_params=params(2 if tight else 24),
    )(far_sum, *far_parts)
    back = exchange(far_out, group)
    base, mix = pl.pallas_call(
        functools.partial(near_kernel, half),
        out_shape=(like(requests, width, dtype=F32), like(requests, count, dtype=F32)),
        in_specs=[whole()] * (4 + chips),
        out_specs=(whole(),) * 2,
        compiler_params=params(2 if tight else 24),
    )(residual, normed, router_weight.T, routes, near_sum, *near_parts)
    return pl.pallas_call(
        mix_kernel,
        out_shape=like(requests, width),
        in_specs=[whole()] * 3,
        out_specs=whole(),
        compiler_params=params(2 if tight else 24),
    )(base, mix, back)


def solution(mesh):
    in_specs = (
        P(("rep", "pool"), None),
        P(("rep", "pool"), None),
        P(("rep", "pool"), None, None),
        P(("rep", "pool"), None, None),
        P(("rep", "pool"), None),
        P(("rep", "pool"), None),
        P(),
        P(),
        P("pool", None, None),
        P("pool", None, None),
        P("pool", None, None),
    )
    out_specs = P(("rep", "pool"), None)
    return jax.shard_map(body, mesh=mesh, in_specs=in_specs, out_specs=out_specs, check_vma=False)
```

```python
import functools
import math

import jax
import jax.numpy as jnp
from jax import lax
from jax.experimental import pallas as pl
from jax.experimental.pallas import tpu as pltpu
from jax.sharding import PartitionSpec as P

HEADS = 48
KV_HEADS = 8
HEAD_DIM = 128
FLIGHT = 2
CORES = 2
EPSILON = 1e-05

F32 = jnp.float32
BF16 = jnp.bfloat16
NT = (((1,), (1,)), ((), ()))
TN = (((0,), (0,)), ((), ()))
MIB = 1 << 20


def whole(space=pltpu.VMEM):
    return pl.BlockSpec(memory_space=space)


def iota(shape, dim):
    return lax.broadcasted_iota(jnp.int32, shape, dim)


def spread(rows):
    n = rows.shape[1]
    return jnp.broadcast_to(rows, (n, n)), iota((n, n), 0), iota((n, n), 1)


def to_column(values):
    wide, row, lane = spread(values)
    return jnp.sum(jnp.where(row == lane, wide, 0.0), axis=1, keepdims=True)


def slot_rows(routes, expert):
    named = jnp.max((routes == expert).astype(F32), axis=0, keepdims=True)
    column = to_column(named)
    _, row, lane = spread(named)
    before = jnp.sum(jnp.where(row < lane, column, 0.0), axis=0, keepdims=True)
    return named, before


def front_kernel(half, hidden_hbm, queries_hbm, cached_hbm, own_hbm, lengths_hbm, routes_hbm, gain_hbm,
                 residual_ref, normed_ref, near_ref, far_ref,
                 hidden_ref, queries_ref, kv_ref, own_ref, lengths_ref, routes_ref, gain_ref, wide_ref, att_ref, sems):
    pairs = (
        (lengths_hbm, lengths_ref),
        (queries_hbm, queries_ref),
        (cached_hbm.reshape(kv_ref.shape), kv_ref),
        (own_hbm.reshape(own_ref.shape), own_ref),
        (hidden_hbm, hidden_ref),
        (gain_hbm, gain_ref),
        (routes_hbm, routes_ref),
    )
    copies = [pltpu.make_async_copy(src, dst, sems.at[i]) for i, (src, dst) in enumerate(pairs)]
    for copy in copies:
        copy.start()
    requests, width = hidden_ref.shape
    groups = HEADS // KV_HEADS
    positions = kv_ref.shape[0]
    scale = 1.0 / math.sqrt(HEAD_DIM)
    row, lane = iota((requests, requests), 0), iota((requests, requests), 1)
    copies[0].wait()
    lengths = jnp.broadcast_to(lengths_ref[...], (requests, requests))
    starts = jnp.sum(jnp.where(lane < row, lengths, 0), axis=1, keepdims=True)
    ends = starts + jnp.sum(jnp.where(lane == row, lengths, 0), axis=1, keepdims=True)
    column = iota((requests, positions), 1)
    inside = (column >= 2 * starts) & (column < 2 * ends) & (column % 2 == 0)
    bias = jnp.where(inside, 0.0, -jnp.inf).astype(F32)
    bias = jnp.concatenate([bias] * groups, axis=0)
    copies[6].wait()
    mine = half()
    slot = iota((near_ref.shape[0], requests), 0).astype(F32)
    placing = []
    for expert in (mine, 1 - mine):
        named, before = slot_rows(routes_ref[...], expert)
        placing.append(jnp.where(before == slot, named, 0.0))
    placing = jnp.concatenate(placing, axis=0).astype(BF16)
    copies[1].wait()
    queries = queries_ref[...].astype(F32)
    copies[3].wait()
    for head in range(KV_HEADS):
        wide_ref[head] = own_ref[:, head * HEAD_DIM:(head + 1) * HEAD_DIM].astype(F32)
    copies[2].wait()
    heads = range(KV_HEADS)
    blocks = [kv_ref[:, head * HEAD_DIM:(head + 1) * HEAD_DIM] for head in heads]
    stacks = []
    for head in heads:
        at = head * groups * HEAD_DIM
        stacks.append(jnp.concatenate([queries[:, at + j * HEAD_DIM:at + (j + 1) * HEAD_DIM] for j in range(groups)], axis=0))
    keys = [jnp.concatenate([wide_ref[head, pl.ds(0, requests, stride=2), :]] * groups, axis=0) for head in heads]
    raw = [lax.dot_general(s.astype(BF16), k, NT, preferred_element_type=F32) for s, k in zip(stacks, blocks)]
    own_scores = [jnp.sum(s * k, axis=1, keepdims=True) * scale for s, k in zip(stacks, keys)]
    weights, own_weights = [], []
    for r, own_score in zip(raw, own_scores):
        scores = r * scale + bias
        peak = jnp.maximum(jnp.max(scores, axis=1, keepdims=True), own_score)
        expos = jnp.exp(scores - peak)
        own_expo = jnp.exp(own_score - peak)
        total = jnp.sum(expos, axis=1, keepdims=True) + own_expo
        weights.append(pltpu.roll(expos / total, 1, 1).astype(BF16))
        own_weights.append((own_expo / total).astype(BF16).astype(F32))
    sums = [jnp.dot(w, k, preferred_element_type=F32) for w, k in zip(weights, blocks)]
    for head, summed, own_weight in zip(heads, sums, own_weights):
        summed = summed + own_weight * jnp.concatenate([wide_ref[head, pl.ds(1, requests, stride=2), :]] * groups, axis=0)
        for j in range(groups):
            at = (head * groups + j) * HEAD_DIM
            att_ref[:, at:at + HEAD_DIM] = summed[j * requests:(j + 1) * requests].astype(BF16).astype(F32)
    copies[4].wait()
    residual = hidden_ref[...].astype(F32) + att_ref[...]
    residual_ref[...] = residual
    centered = residual - jnp.mean(residual, axis=1, keepdims=True)
    spread_of = jnp.mean(centered * centered, axis=1, keepdims=True)
    copies[5].wait()
    normed = (centered * lax.rsqrt(spread_of + EPSILON) * gain_ref[...]).astype(BF16)
    normed_ref[...] = normed
    capacity = near_ref.shape[0]
    packed = jnp.dot(placing, normed, preferred_element_type=F32).astype(BF16)
    near_ref[...] = packed[:capacity]
    far_ref[...] = packed[capacity:]


def gate_mix(half, normed_ref, router_ref, routes_ref, capacity):
    routes = routes_ref[...]
    fanout, requests = routes.shape
    experts = router_ref.shape[0]
    logits = lax.dot_general(normed_ref[...], router_ref[...], NT, preferred_element_type=F32)
    lane = iota((requests, experts), 1).astype(F32)
    columns = [to_column(routes[k:k + 1].astype(F32)) for k in range(fanout)]
    routed = [jnp.sum(jnp.where(lane == columns[k], logits, 0.0), axis=1, keepdims=True) for k in range(fanout)]
    gates = [1.0 / sum(jnp.exp(routed[j] - routed[k]) for j in range(fanout)) for k in range(fanout)]
    mine = half()
    column = iota((requests, FLIGHT * capacity), 1)
    mix = jnp.zeros((requests, FLIGHT * capacity), F32)
    for turn, expert in enumerate((mine, 1 - mine)):
        named, before = slot_rows(routes, expert)
        named, before = to_column(named), to_column(before)
        gate = jnp.zeros((requests, 1), F32)
        for k in range(fanout):
            gate = jnp.where(columns[k] == expert.astype(F32), gates[k], gate)
        place = (column - turn * capacity).astype(F32)
        mix = jnp.where((before == place) & (named > 0.0), gate, mix)
    return mix


def join_kernel(near_ref, arrived_ref, out_ref):
    out_ref[...] = jnp.concatenate([near_ref[...], arrived_ref[...]], axis=0)


def project(inner_ref, down_ref, keep_ref, send_ref, start):
    rows = inner_ref[...]
    half = rows.shape[0] // 2
    doubled = jnp.concatenate([rows, rows], axis=0)
    width = keep_ref.shape[1]
    part = 1024 if width % 1024 == 0 else width
    for i in range(width // part):
        at = slice(i * part, (i + 1) * part)
        out = jnp.dot(doubled, down_ref[:, start + i * part:start + (i + 1) * part], preferred_element_type=F32)
        keep_ref[:, at] = out[:half]
        send_ref[:, at] = out[half:2 * half].astype(BF16)


def expert_kernel(chips, chunk, depth, *refs):
    pieces = refs[:2 * chips]
    gate_ref, up_ref, inner_ref, rows_ref = refs[2 * chips:]
    hidden, width = gate_ref.shape
    count = pieces[0].shape[0]
    for i, piece in enumerate(pieces):
        rows_ref[i * count:(i + 1) * count, :] = piece[...]
    for i in range(hidden // chunk):
        at = slice(i * chunk, (i + 1) * chunk)
        gate_part = jnp.zeros((rows_ref.shape[0], chunk), F32)
        up_part = jnp.zeros((chunk, rows_ref.shape[0]), F32)
        for k in range(0, width, depth):
            rows = rows_ref[:, k:k + depth]
            gate_part += lax.dot_general(rows, gate_ref[at, k:k + depth], NT, preferred_element_type=F32)
            up_part += lax.dot_general(up_ref[at, k:k + depth], rows, NT, preferred_element_type=F32)
        inner_ref[:, at] = (gate_part / (1.0 + jnp.exp(-gate_part)) * up_part.T).astype(BF16)


def rest_kernel(start, inner_ref, down_ref, keep_ref, send_ref):
    project(inner_ref, down_ref, keep_ref, send_ref, start)


def core_sum_kernel(keep_ref, recv_ref, near_ref, far_ref, *rest):
    capacity = near_ref.shape[0]
    start = keep_ref.shape[1]
    for keep, recv, at in ((keep_ref, recv_ref, slice(0, start)),):
        total = keep[...] + recv[...].astype(F32)
        for i, out in enumerate((near_ref, far_ref) + rest):
            out[:, at] = total[i * capacity:(i + 1) * capacity].astype(out.dtype)


def far_sum_kernel(far_ref, *refs):
    *parts, out_ref = refs
    total = far_ref[...]
    for part in parts:
        total = total + part[...].astype(F32)
    out_ref[...] = total.astype(BF16)


def weighted(mix, rows, start):
    terms = [mix[:, start + j:start + j + 1] * rows[j:j + 1] for j in range(rows.shape[0])]
    return sum(terms[1:], terms[0])


def near_kernel(half, residual_ref, normed_ref, router_ref, routes_ref, near_ref, *refs):
    *parts, base_ref, mix_ref = refs
    mix = gate_mix(half, normed_ref, router_ref, routes_ref, near_ref.shape[0])
    mix_ref[...] = mix
    total = near_ref[...]
    for part in parts:
        total = total + part[...].astype(F32)
    base_ref[...] = residual_ref[...] + weighted(mix, total.astype(BF16).astype(F32), 0)


def mix_kernel(base_ref, mix_ref, far_ref, out_hbm, out_ref, sems):
    mix = mix_ref[...]
    width = base_ref.shape[1]
    part = width // 3 // 128 * 128
    copies = []
    for i, start in enumerate(range(0, width, part)):
        at = pl.ds(start, part)
        rows = far_ref[:, at].astype(F32)
        out_ref[:, at] = (base_ref[:, at] + weighted(mix, rows, rows.shape[0])).astype(BF16)
        copies.append(pltpu.make_async_copy(out_ref.at[:, at], out_hbm.at[:, at], sems.at[i]))
        copies[-1].start()
    for copy in copies:
        copy.wait()


def like(*shape, dtype=BF16):
    return jax.ShapeDtypeStruct(shape, dtype)


def params(mib):
    return pltpu.CompilerParams(vmem_limit_bytes=mib * MIB)


def body(
    hidden_state,
    queries,
    new_entries,
    cached,
    cache_lengths,
    routes,
    norm_gain,
    router_weight,
    expert_gate,
    expert_up,
    expert_down,
):
    requests, width = hidden_state.shape
    devices = lax.axis_size("pool")
    group = devices // FLIGHT
    chips = group // CORES
    experts = router_weight.shape[1]
    fanout = routes.shape[1]
    capacity = min(requests, 2 * requests * fanout // experts)
    count = 2 * capacity
    hidden = expert_gate.shape[2]

    tight = 6 * hidden * width > 24 * MIB

    def half():
        return lax.axis_index("pool") // group

    def exchange(value, bit):
        return lax.ppermute(value, "pool", [(i, i ^ bit) for i in range(devices)])

    positions = cached.shape[0]
    heads = cached.shape[2]
    weights = [
        pltpu.with_memory_space_constraint(w, pltpu.VMEM)
        for w in (jnp.swapaxes(expert_gate, 1, 2)[0], jnp.swapaxes(expert_up, 1, 2)[0], expert_down[0])
    ]
    routes = routes.T
    front = (hidden_state, queries, cached, new_entries, cache_lengths, routes, norm_gain[None])
    residual, normed, near, far = pl.pallas_call(
        functools.partial(front_kernel, half),
        out_shape=(like(requests, width, dtype=F32), like(requests, width), like(capacity, width), like(capacity, width)),
        in_specs=[whole(pltpu.HBM)] * 7,
        out_specs=(whole(),) * 4,
        scratch_shapes=[
            pltpu.VMEM((requests, width), BF16),
            pltpu.VMEM((requests, width), BF16),
            pltpu.VMEM((2 * positions, heads), BF16),
            pltpu.VMEM((2 * requests, heads), BF16),
            pltpu.VMEM((1, requests), jnp.int32),
            pltpu.VMEM((fanout, requests), jnp.int32),
            pltpu.VMEM((1, width), F32),
            pltpu.VMEM((KV_HEADS, 2 * requests, HEAD_DIM), F32),
            pltpu.VMEM((requests, width), F32),
            pltpu.SemaphoreType.DMA((7,)),
        ],
        compiler_params=params(2 if tight else 24),
        cost_estimate=pl.CostEstimate(flops=200_000_000_000, bytes_accessed=50_000_000, transcendentals=0),
    )(*(pltpu.with_memory_space_constraint(x, pltpu.HBM) for x in front))
    arrived = exchange(far, group)
    own = pl.pallas_call(
        join_kernel,
        out_shape=like(count, width),
        in_specs=[whole()] * 2,
        out_specs=whole(),
        compiler_params=params(2 if tight else 24),
    )(near, arrived)
    mine = [own] + [exchange(own, CORES * j) for j in range(1, chips)]
    beside = [exchange(piece, 1) for piece in mine]
    chunk = 336 if hidden % 336 == 0 else hidden
    depth = 256 if width % 256 == 0 else width
    rows = chips * count
    start = 2 * width // 3 // 1024 * 1024
    inner = pl.pallas_call(
        functools.partial(expert_kernel, chips, chunk, depth),
        out_shape=like(2 * rows, hidden),
        in_specs=[whole()] * (2 * chips + 2),
        out_specs=whole(),
        scratch_shapes=[pltpu.VMEM((2 * rows, width), BF16)],
        compiler_params=params(2 if tight else 24),
    )(*mine, *beside, *weights[:2])

    def down(start, columns):
        return pl.pallas_call(
            functools.partial(rest_kernel, start),
            out_shape=(like(rows, columns, dtype=F32), like(rows, columns)),
            in_specs=[whole()] * 2,
            out_specs=(whole(),) * 2,
            compiler_params=params(2 if tight else 24),
        )(inner, weights[2])

    keep, send = down(0, width)
    recv = exchange(send, 1)
    in_vmem = [pltpu.with_memory_space_constraint(x, pltpu.VMEM) for x in (keep, recv)]
    near_sum, far_sum, *rest = pl.pallas_call(
        core_sum_kernel,
        out_shape=(like(capacity, width, dtype=F32),) * 2 + (like(capacity, width),) * (2 * chips - 2),
        in_specs=[whole()] * 2,
        out_specs=(whole(),) * (2 * chips),
        compiler_params=params(2 if tight else 24),
    )(*in_vmem)
    order = range(chips - 1, 0, -1)
    far_parts = [exchange(rest[2 * j - 1], CORES * j) for j in order]
    near_parts = [exchange(rest[2 * j - 2], CORES * j) for j in order]
    far_out = pl.pallas_call(
        far_sum_kernel,
        out_shape=like(capacity, width),
        in_specs=[whole()] * chips,
        out_specs=whole(),
        compiler_params=params(2 if tight else 24),
    )(far_sum, *far_parts)
    back = exchange(far_out, group)
    base, mix = pl.pallas_call(
        functools.partial(near_kernel, half),
        out_shape=(like(requests, width, dtype=F32), like(requests, count, dtype=F32)),
        in_specs=[whole()] * (4 + chips),
        out_specs=(whole(),) * 2,
        compiler_params=params(2 if tight else 24),
    )(residual, normed, router_weight.T, routes, near_sum, *near_parts)
    return pl.pallas_call(
        mix_kernel,
        out_shape=like(requests, width),
        in_specs=[whole()] * 3,
        out_specs=whole(pltpu.HBM),
        scratch_shapes=[pltpu.VMEM((requests, width), BF16), pltpu.SemaphoreType.DMA((3,))],
        compiler_params=params(2 if tight else 24),
    )(base, mix, back)


def solution(mesh):
    in_specs = (
        P(("rep", "pool"), None),
        P(("rep", "pool"), None),
        P(("rep", "pool"), None, None),
        P(("rep", "pool"), None, None),
        P(("rep", "pool"), None),
        P(("rep", "pool"), None),
        P(),
        P(),
        P("pool", None, None),
        P("pool", None, None),
        P("pool", None, None),
    )
    out_specs = P(("rep", "pool"), None)
    return jax.shard_map(body, mesh=mesh, in_specs=in_specs, out_specs=out_specs, check_vma=False)
```

```python
import functools
import math

import jax
import jax.numpy as jnp
from jax import lax
from jax.experimental import pallas as pl
from jax.experimental.pallas import tpu as pltpu
from jax.sharding import PartitionSpec as P

HEADS = 48
KV_HEADS = 8
HEAD_DIM = 128
FLIGHT = 2
CORES = 2
EPSILON = 1e-05

F32 = jnp.float32
BF16 = jnp.bfloat16
NT = (((1,), (1,)), ((), ()))
TN = (((0,), (0,)), ((), ()))
MIB = 1 << 20


def whole(space=pltpu.VMEM):
    return pl.BlockSpec(memory_space=space)


def iota(shape, dim):
    return lax.broadcasted_iota(jnp.int32, shape, dim)


def spread(rows):
    n = rows.shape[1]
    return jnp.broadcast_to(rows, (n, n)), iota((n, n), 0), iota((n, n), 1)


def to_column(values):
    wide, row, lane = spread(values)
    return jnp.sum(jnp.where(row == lane, wide, 0.0), axis=1, keepdims=True)


def slot_rows(routes, expert):
    named = jnp.max((routes == expert).astype(F32), axis=0, keepdims=True)
    column = to_column(named)
    _, row, lane = spread(named)
    before = jnp.sum(jnp.where(row < lane, column, 0.0), axis=0, keepdims=True)
    return named, before


def front_kernel(half, hidden_hbm, queries_hbm, cached_hbm, own_hbm, lengths_hbm, routes_hbm, gain_hbm,
                 residual_ref, normed_ref, near_ref, far_ref,
                 hidden_ref, queries_ref, kv_ref, own_ref, lengths_ref, routes_ref, gain_ref, wide_ref, att_ref, sems):
    pairs = (
        (lengths_hbm, lengths_ref),
        (queries_hbm, queries_ref),
        (cached_hbm.reshape(kv_ref.shape), kv_ref),
        (own_hbm.reshape(own_ref.shape), own_ref),
        (hidden_hbm, hidden_ref),
        (gain_hbm, gain_ref),
        (routes_hbm, routes_ref),
    )
    copies = [pltpu.make_async_copy(src, dst, sems.at[i]) for i, (src, dst) in enumerate(pairs)]
    for copy in copies:
        copy.start()
    requests, width = hidden_ref.shape
    groups = HEADS // KV_HEADS
    positions = kv_ref.shape[0]
    scale = 1.0 / math.sqrt(HEAD_DIM)
    row, lane = iota((requests, requests), 0), iota((requests, requests), 1)
    copies[0].wait()
    lengths = jnp.broadcast_to(lengths_ref[...], (requests, requests))
    starts = jnp.sum(jnp.where(lane < row, lengths, 0), axis=1, keepdims=True)
    ends = starts + jnp.sum(jnp.where(lane == row, lengths, 0), axis=1, keepdims=True)
    column = iota((requests, positions), 1)
    inside = (column >= 2 * starts) & (column < 2 * ends) & (column % 2 == 0)
    bias = jnp.where(inside, 0.0, -jnp.inf).astype(F32)
    bias = jnp.concatenate([bias] * groups, axis=0)
    copies[6].wait()
    mine = half()
    slot = iota((near_ref.shape[0], requests), 0).astype(F32)
    placing = []
    for expert in (mine, 1 - mine):
        named, before = slot_rows(routes_ref[...], expert)
        placing.append(jnp.where(before == slot, named, 0.0))
    placing = jnp.concatenate(placing, axis=0).astype(BF16)
    copies[1].wait()
    queries = queries_ref[...].astype(F32)
    copies[3].wait()
    for head in range(KV_HEADS):
        wide_ref[head] = own_ref[:, head * HEAD_DIM:(head + 1) * HEAD_DIM].astype(F32)
    copies[2].wait()
    heads = range(KV_HEADS)
    blocks = [kv_ref[:, head * HEAD_DIM:(head + 1) * HEAD_DIM] for head in heads]
    stacks = []
    for head in heads:
        at = head * groups * HEAD_DIM
        stacks.append(jnp.concatenate([queries[:, at + j * HEAD_DIM:at + (j + 1) * HEAD_DIM] for j in range(groups)], axis=0))
    keys = [jnp.concatenate([wide_ref[head, pl.ds(0, requests, stride=2), :]] * groups, axis=0) for head in heads]
    raw = [lax.dot_general(s.astype(BF16), k, NT, preferred_element_type=F32) for s, k in zip(stacks, blocks)]
    own_scores = [jnp.sum(s * k, axis=1, keepdims=True) * scale for s, k in zip(stacks, keys)]
    weights, own_weights = [], []
    for r, own_score in zip(raw, own_scores):
        scores = r * scale + bias
        peak = jnp.maximum(jnp.max(scores, axis=1, keepdims=True), own_score)
        expos = jnp.exp(scores - peak)
        own_expo = jnp.exp(own_score - peak)
        total = jnp.sum(expos, axis=1, keepdims=True) + own_expo
        weights.append(pltpu.roll(expos / total, 1, 1).astype(BF16))
        own_weights.append((own_expo / total).astype(BF16).astype(F32))
    sums = [jnp.dot(w, k, preferred_element_type=F32) for w, k in zip(weights, blocks)]
    for head, summed, own_weight in zip(heads, sums, own_weights):
        summed = summed + own_weight * jnp.concatenate([wide_ref[head, pl.ds(1, requests, stride=2), :]] * groups, axis=0)
        for j in range(groups):
            at = (head * groups + j) * HEAD_DIM
            att_ref[:, at:at + HEAD_DIM] = summed[j * requests:(j + 1) * requests].astype(BF16).astype(F32)
    copies[4].wait()
    residual = hidden_ref[...].astype(F32) + att_ref[...]
    residual_ref[...] = residual
    centered = residual - jnp.mean(residual, axis=1, keepdims=True)
    spread_of = jnp.mean(centered * centered, axis=1, keepdims=True)
    copies[5].wait()
    normed = (centered * lax.rsqrt(spread_of + EPSILON) * gain_ref[...]).astype(BF16)
    normed_ref[...] = normed
    capacity = near_ref.shape[0]
    packed = jnp.dot(placing, normed, preferred_element_type=F32).astype(BF16)
    near_ref[...] = packed[:capacity]
    far_ref[...] = packed[capacity:]


def gate_mix(half, normed_ref, router_ref, routes_ref, capacity):
    routes = routes_ref[...]
    fanout, requests = routes.shape
    experts = router_ref.shape[0]
    logits = lax.dot_general(normed_ref[...], router_ref[...], NT, preferred_element_type=F32)
    lane = iota((requests, experts), 1).astype(F32)
    columns = [to_column(routes[k:k + 1].astype(F32)) for k in range(fanout)]
    routed = [jnp.sum(jnp.where(lane == columns[k], logits, 0.0), axis=1, keepdims=True) for k in range(fanout)]
    gates = [1.0 / sum(jnp.exp(routed[j] - routed[k]) for j in range(fanout)) for k in range(fanout)]
    mine = half()
    column = iota((requests, FLIGHT * capacity), 1)
    mix = jnp.zeros((requests, FLIGHT * capacity), F32)
    for turn, expert in enumerate((mine, 1 - mine)):
        named, before = slot_rows(routes, expert)
        named, before = to_column(named), to_column(before)
        gate = jnp.zeros((requests, 1), F32)
        for k in range(fanout):
            gate = jnp.where(columns[k] == expert.astype(F32), gates[k], gate)
        place = (column - turn * capacity).astype(F32)
        mix = jnp.where((before == place) & (named > 0.0), gate, mix)
    return mix


def join_kernel(near_ref, arrived_ref, out_ref):
    out_ref[...] = jnp.concatenate([near_ref[...], arrived_ref[...]], axis=0)


def project(inner_ref, down_ref, keep_ref, *sends):
    rows = inner_ref[...]
    half = rows.shape[0] // 2
    each = half // len(sends)
    doubled = jnp.concatenate([rows, rows], axis=0)
    width = keep_ref.shape[1]
    part = 1024 if width % 1024 == 0 else width
    for i in range(width // part):
        at = slice(i * part, (i + 1) * part)
        out = jnp.dot(doubled, down_ref[:, at], preferred_element_type=F32)
        keep_ref[:, at] = out[:half]
        for j, send in enumerate(sends):
            send[:, at] = out[half + j * each:half + (j + 1) * each].astype(BF16)


def expert_kernel(chips, chunk, depth, *refs):
    pieces = refs[:2 * chips]
    gate_ref, up_ref, inner_ref, rows_ref = refs[2 * chips:]
    hidden, width = gate_ref.shape
    count = pieces[0].shape[0]
    for i, piece in enumerate(pieces):
        rows_ref[i * count:(i + 1) * count, :] = piece[...]
    for i in range(hidden // chunk):
        at = slice(i * chunk, (i + 1) * chunk)
        gate_part = jnp.zeros((rows_ref.shape[0], chunk), F32)
        up_part = jnp.zeros((chunk, rows_ref.shape[0]), F32)
        for k in range(0, width, depth):
            rows = rows_ref[:, k:k + depth]
            gate_part += lax.dot_general(rows, gate_ref[at, k:k + depth], NT, preferred_element_type=F32)
            up_part += lax.dot_general(up_ref[at, k:k + depth], rows, NT, preferred_element_type=F32)
        inner_ref[:, at] = (gate_part / (1.0 + jnp.exp(-gate_part)) * up_part.T).astype(BF16)


def core_sum_kernel(split, keep_ref, *refs):
    received, outs = refs[:split], refs[split:]
    capacity = outs[0].shape[0]
    each = received[0].shape[0]
    for j, recv in enumerate(received):
        total = keep_ref[j * each:(j + 1) * each] + recv[...].astype(F32)
        for i in range(each // capacity):
            out = outs[j * (each // capacity) + i]
            out[...] = total[i * capacity:(i + 1) * capacity].astype(out.dtype)


def far_sum_kernel(far_ref, *refs):
    *parts, out_ref = refs
    total = far_ref[...]
    for part in parts:
        total = total + part[...].astype(F32)
    out_ref[...] = total.astype(BF16)


def weighted(mix, rows, start):
    terms = [mix[:, start + j:start + j + 1] * rows[j:j + 1] for j in range(rows.shape[0])]
    return sum(terms[1:], terms[0])


def near_kernel(half, residual_ref, normed_ref, router_ref, routes_ref, near_ref, *refs):
    *parts, base_ref, mix_ref = refs
    mix = gate_mix(half, normed_ref, router_ref, routes_ref, near_ref.shape[0])
    mix_ref[...] = mix
    total = near_ref[...]
    for part in parts:
        total = total + part[...].astype(F32)
    base_ref[...] = residual_ref[...] + weighted(mix, total.astype(BF16).astype(F32), 0)


def mix_kernel(base_ref, mix_ref, far_ref, out_hbm, out_ref, sems):
    mix = mix_ref[...]
    width = base_ref.shape[1]
    part = width // 3 // 128 * 128
    copies = []
    for i, start in enumerate(range(0, width, part)):
        at = pl.ds(start, part)
        rows = far_ref[:, at].astype(F32)
        out_ref[:, at] = (base_ref[:, at] + weighted(mix, rows, rows.shape[0])).astype(BF16)
        copies.append(pltpu.make_async_copy(out_ref.at[:, at], out_hbm.at[:, at], sems.at[i]))
        copies[-1].start()
    for copy in copies:
        copy.wait()


def like(*shape, dtype=BF16):
    return jax.ShapeDtypeStruct(shape, dtype)


def params(mib):
    return pltpu.CompilerParams(vmem_limit_bytes=mib * MIB)


def body(
    hidden_state,
    queries,
    new_entries,
    cached,
    cache_lengths,
    routes,
    norm_gain,
    router_weight,
    expert_gate,
    expert_up,
    expert_down,
):
    requests, width = hidden_state.shape
    devices = lax.axis_size("pool")
    group = devices // FLIGHT
    chips = group // CORES
    experts = router_weight.shape[1]
    fanout = routes.shape[1]
    capacity = min(requests, 2 * requests * fanout // experts)
    count = 2 * capacity
    hidden = expert_gate.shape[2]

    tight = 6 * hidden * width > 24 * MIB

    def half():
        return lax.axis_index("pool") // group

    def exchange(value, bit):
        return lax.ppermute(value, "pool", [(i, i ^ bit) for i in range(devices)])

    positions = cached.shape[0]
    heads = cached.shape[2]
    weights = [
        pltpu.with_memory_space_constraint(w, pltpu.VMEM)
        for w in (jnp.swapaxes(expert_gate, 1, 2)[0], jnp.swapaxes(expert_up, 1, 2)[0], expert_down[0])
    ]
    routes = routes.T
    front = (hidden_state, queries, cached, new_entries, cache_lengths, routes, norm_gain[None])
    residual, normed, near, far = pl.pallas_call(
        functools.partial(front_kernel, half),
        out_shape=(like(requests, width, dtype=F32), like(requests, width), like(capacity, width), like(capacity, width)),
        in_specs=[whole(pltpu.HBM)] * 7,
        out_specs=(whole(),) * 4,
        scratch_shapes=[
            pltpu.VMEM((requests, width), BF16),
            pltpu.VMEM((requests, width), BF16),
            pltpu.VMEM((2 * positions, heads), BF16),
            pltpu.VMEM((2 * requests, heads), BF16),
            pltpu.VMEM((1, requests), jnp.int32),
            pltpu.VMEM((fanout, requests), jnp.int32),
            pltpu.VMEM((1, width), F32),
            pltpu.VMEM((KV_HEADS, 2 * requests, HEAD_DIM), F32),
            pltpu.VMEM((requests, width), F32),
            pltpu.SemaphoreType.DMA((7,)),
        ],
        compiler_params=params(2 if tight else 24),
        cost_estimate=pl.CostEstimate(flops=200_000_000_000, bytes_accessed=50_000_000, transcendentals=0),
    )(*(pltpu.with_memory_space_constraint(x, pltpu.HBM) for x in front))
    arrived = exchange(far, group)
    own = pl.pallas_call(
        join_kernel,
        out_shape=like(count, width),
        in_specs=[whole()] * 2,
        out_specs=whole(),
        compiler_params=params(2 if tight else 24),
    )(near, arrived)
    mine = [own] + [exchange(own, CORES * j) for j in range(1, chips)]
    beside = [exchange(piece, 1) for piece in mine]
    chunk = 336 if hidden % 336 == 0 else hidden
    depth = 256 if width % 256 == 0 else width
    rows = chips * count
    inner = pl.pallas_call(
        functools.partial(expert_kernel, chips, chunk, depth),
        out_shape=like(2 * rows, hidden),
        in_specs=[whole()] * (2 * chips + 2),
        out_specs=whole(),
        scratch_shapes=[pltpu.VMEM((2 * rows, width), BF16)],
        compiler_params=params(2 if tight else 24),
    )(*mine, *beside, *weights[:2])

    split = 2
    keep, *sends = pl.pallas_call(
        project,
        out_shape=(like(rows, width, dtype=F32),) + (like(rows // split, width),) * split,
        in_specs=[whole()] * 2,
        out_specs=(whole(),) * (1 + split),
        compiler_params=params(2 if tight else 24),
    )(inner, weights[2])
    received = [exchange(send, 1) for send in sends]
    in_vmem = [pltpu.with_memory_space_constraint(x, pltpu.VMEM) for x in (keep, *received)]
    near_sum, far_sum, *rest = pl.pallas_call(
        functools.partial(core_sum_kernel, split),
        out_shape=(like(capacity, width, dtype=F32),) * 2 + (like(capacity, width),) * (2 * chips - 2),
        in_specs=[whole()] * (1 + split),
        out_specs=(whole(),) * (2 * chips),
        compiler_params=params(2 if tight else 24),
    )(*in_vmem)
    order = range(chips - 1, 0, -1)
    far_parts = [exchange(rest[2 * j - 1], CORES * j) for j in order]
    near_parts = [exchange(rest[2 * j - 2], CORES * j) for j in order]
    far_out = pl.pallas_call(
        far_sum_kernel,
        out_shape=like(capacity, width),
        in_specs=[whole()] * chips,
        out_specs=whole(),
        compiler_params=params(2 if tight else 24),
    )(far_sum, *far_parts)
    back = exchange(far_out, group)
    base, mix = pl.pallas_call(
        functools.partial(near_kernel, half),
        out_shape=(like(requests, width, dtype=F32), like(requests, count, dtype=F32)),
        in_specs=[whole()] * (4 + chips),
        out_specs=(whole(),) * 2,
        compiler_params=params(2 if tight else 24),
    )(residual, normed, router_weight.T, routes, near_sum, *near_parts)
    return pl.pallas_call(
        mix_kernel,
        out_shape=like(requests, width),
        in_specs=[whole()] * 3,
        out_specs=whole(pltpu.HBM),
        scratch_shapes=[pltpu.VMEM((requests, width), BF16), pltpu.SemaphoreType.DMA((3,))],
        compiler_params=params(2 if tight else 24),
    )(base, mix, back)


def solution(mesh):
    in_specs = (
        P(("rep", "pool"), None),
        P(("rep", "pool"), None),
        P(("rep", "pool"), None, None),
        P(("rep", "pool"), None, None),
        P(("rep", "pool"), None),
        P(("rep", "pool"), None),
        P(),
        P(),
        P("pool", None, None),
        P("pool", None, None),
        P("pool", None, None),
    )
    out_specs = P(("rep", "pool"), None)
    return jax.shard_map(body, mesh=mesh, in_specs=in_specs, out_specs=out_specs, check_vma=False)
```
